512 devices in a mesh: dp: 4 (over y), seq: 128 (over x, z, core).
Axes of the slice: x: 4, y: 4, z: 16, core: 2. Of those that a mesh axis runs over, the one named last changes fastest.
Arguments:
- queries: bfloat16 [4, 16384, 1792], P('dp', 'seq'), may hold values from -132 to 132, as said below
- keys: bfloat16 [4, 16384, 256], P('dp', 'seq'), may hold values from -6 to 6, as said below
- values: bfloat16 [4, 16384, 256], P('dp', 'seq'), may hold values from -6 to 6
- grad_out: bfloat16 [4, 16384, 1792], P('dp', 'seq'), may hold values from -24 to 24
- beacon_keys: bfloat16 [4, 1024, 256], P('dp', 'seq'), may hold values from -6 to 6
- beacon_values: bfloat16 [4, 1024, 256], P('dp', 'seq'), may hold values from -6 to 6
- beacon_hidden: bfloat16 [4, 1024, 3584], P('dp', 'seq'), may hold values from -6 to 6
- order: int32 [128], replicated, may hold values from 0 to 127, each once
- ratio: int32 [128], replicated, may hold values from 16 to 32, as said below
Outputs:
- query_grads: bfloat16 [4, 16384, 1792], P('dp', 'seq')
- key_grads: bfloat16 [4, 16384, 256], P('dp', 'seq')
- value_grads: bfloat16 [4, 16384, 256], P('dp', 'seq')
- beacon_key_grads: bfloat16 [4, 1024, 256], P('dp', 'seq')
- beacon_value_grads: bfloat16 [4, 1024, 256], P('dp', 'seq')
- key_weight_grad: float32 [3584, 256], P(('dp', 'seq'))
The draws below stay inside these ranges and needn't reach their ends.
Inputs may be any that keep to these rules, and one draw needn't show every extreme that they name: queries lie in this range. keys lie in this range. `ratio`: each entry is 16 or 32, and both occur. `order`: a permutation of 0 to 127.
All inputs are finite; a program needn't handle non-finite values.
Results may differ from the reference program's by a relative error of at most 0.012.
Values may be sent and summed in bfloat16 or wider, within the bound.
No kernel may reach another device: no remote copies, remote signals or barrier semaphores. Data moves between devices by JAX's collectives and lax.ppermute only.
A program may use at most 64 MiB of HBM per device.

```python
import math
import jax
import jax.numpy as jnp
from jax import lax

D = 3584
QH = 14
KVH = 2
HD = 128
SPAN = 128
NBMAX = 8
TOKENS = 16384
BEACONS = 1024
DOCS = 4
N_DP = 4
N_SEQ = 128


def base_keys(key):
    return jnp.clip(jax.random.normal(key, (N_DP, TOKENS, KVH * HD), jnp.float32), -6.0, 6.0)


def draw_keys(key, part):
    shared = base_keys(key)
    return shared.astype(jnp.bfloat16)


def draw_queries(key, part):
    key = jax.random.fold_in(key, 5)
    fresh = jnp.clip(jax.random.normal(key, (N_DP, TOKENS, QH * HD), jnp.float32), -6.0, 6.0)
    return fresh.astype(jnp.bfloat16)


def draw_ratio(key, part):
    key = jax.random.fold_in(key, 11)
    picked = 16 * (1 + jax.random.randint(key, (N_SEQ,), 0, 2, dtype=jnp.int32))
    index = jnp.arange(N_SEQ, dtype=jnp.int32)
    picked = jnp.where(index == 0, 16, jnp.where(index == 1, 32, picked))
    return picked.astype(jnp.int32)


def block_levels(own_key, extent, cuts, least, top_value):
    gain, own = 1.0, jax.random.fold_in(own_key, 6)
    for position, blocks in cuts:
        heights = jnp.exp(jax.random.uniform(jax.random.fold_in(own, position), (blocks,), jnp.float32, least / len(cuts), top_value / len(cuts)))
        gain = gain * jnp.repeat(heights, extent[position] // blocks).reshape([-1 if axis == position else 1 for axis in range(len(extent))])
    return gain


def bell_draw(own_key, dims, scale, limit, split=(), kind=jnp.bfloat16):
    drawn = jax.random.normal(own_key, dims, jnp.float32) * scale
    if len(split) > 0:
        drawn = block_levels(own_key, dims, split, -0.22, 0.18) * drawn
    return jnp.clip(drawn, min=-limit, max=limit).astype(kind)


def setup_inputs(seed: int = 0) -> dict:
    key_list = jax.random.split(jax.random.key(seed), 10)
    return {
        "queries": draw_queries(jax.random.fold_in(key_list[9], 71), 0),
        "keys": draw_keys(jax.random.fold_in(key_list[9], 71), 0),
        "values": bell_draw(key_list[2], (DOCS, TOKENS, KVH * HD), 1.0, 6.0, ((0, 4), (1, 128))),
        "grad_out": bell_draw(key_list[3], (DOCS, TOKENS, QH * HD), 4.0, 24.0, ((0, 4), (1, 128))),
        "beacon_keys": bell_draw(key_list[4], (DOCS, BEACONS, KVH * HD), 1.0, 6.0, ((0, 4), (1, 128))),
        "beacon_values": bell_draw(key_list[5], (DOCS, BEACONS, KVH * HD), 1.0, 6.0, ((0, 4), (1, 128))),
        "beacon_hidden": bell_draw(key_list[6], (DOCS, BEACONS, D), 1.0, 6.0, ((0, 4), (1, 128))),
        "order": jax.random.permutation(key_list[7], N_SEQ).astype(jnp.int32),
        "ratio": draw_ratio(jax.random.fold_in(key_list[9], 71), 0),
    }


NEG = -1e+30

def to_bf16_f32(array):
    rounded = lax.optimization_barrier(array.astype(jnp.bfloat16))
    return rounded.astype(jnp.float32)

def reference(queries, keys, values, grad_out, beacon_keys, beacon_values, beacon_hidden, order, ratio):
    scale = 1.0 / math.sqrt(HD)
    groups = QH // KVH
    total = N_SEQ * NBMAX
    rows = jnp.arange(total, dtype=jnp.int32)
    owner = rows // NBMAX
    owner_span = order[owner]
    live_slots = SPAN // ratio[owner_span]
    positions = jnp.arange(SPAN, dtype=jnp.int32)
    causal = positions[:, None] >= positions[None, :]
    q_all, k_all, v_all, bk_all, bv_all = ([], [], [], [], [])
    weight_grad = jnp.zeros((D, KVH * HD), jnp.float32)
    for doc in range(N_DP):
        beacon_k = beacon_keys[doc].astype(jnp.float32).reshape(total, KVH, HD)
        beacon_v = beacon_values[doc].astype(jnp.float32).reshape(total, KVH, HD)

        def one_span(acc, block):
            start = (block * SPAN).astype(jnp.int32)
            query = lax.dynamic_slice_in_dim(queries[doc], start, SPAN, 0).astype(jnp.float32).reshape(SPAN, KVH, groups, HD)
            upstream = lax.dynamic_slice_in_dim(grad_out[doc], start, SPAN, 0).astype(jnp.float32).reshape(SPAN, KVH, groups, HD)
            local_k = lax.dynamic_slice_in_dim(keys[doc], start, SPAN, 0).astype(jnp.float32).reshape(SPAN, KVH, HD)
            local_v = lax.dynamic_slice_in_dim(values[doc], start, SPAN, 0).astype(jnp.float32).reshape(SPAN, KVH, HD)
            every_k = jnp.concatenate([local_k, beacon_k], axis=0)
            every_v = jnp.concatenate([local_v, beacon_v], axis=0)
            mine = order[block]
            seen = (owner_span < mine) & (rows % NBMAX < live_slots)
            mask = jnp.concatenate([causal, jnp.broadcast_to(seen[None, :], (SPAN, total))], axis=1)
            scores = jnp.einsum('ikgd,jkd->kgij', query, every_k) * scale
            scores = jnp.where(mask, scores, NEG)
            top = lax.optimization_barrier(jnp.max(scores, axis=-1))
            mass = lax.optimization_barrier(jnp.sum(jnp.exp(scores - top[..., None]), axis=-1))
            lse = top + jnp.log(mass)
            probs = jnp.where(mask, jnp.exp(scores - lse[..., None]), 0.0)
            dprobs = jnp.einsum('ikgd,jkd->kgij', upstream, every_v)
            delta = lax.optimization_barrier(jnp.sum(probs * dprobs, axis=-1))
            dscores = to_bf16_f32(probs * (dprobs - delta[..., None]))
            probs_b = to_bf16_f32(probs)
            dq = jnp.einsum('kgij,jkd->ikgd', dscores, every_k) * scale
            dk = jnp.einsum('kgij,ikgd->jkd', dscores, query) * scale
            dv = jnp.einsum('kgij,ikgd->jkd', probs_b, upstream)
            acc = (acc[0] + dk[SPAN:], acc[1] + dv[SPAN:])
            outs = (dq.reshape(SPAN, QH * HD).astype(jnp.bfloat16), dk[:SPAN].reshape(SPAN, KVH * HD).astype(jnp.bfloat16), dv[:SPAN].reshape(SPAN, KVH * HD).astype(jnp.bfloat16))
            return (acc, outs)
        init = (jnp.zeros((total, KVH, HD), jnp.float32), jnp.zeros((total, KVH, HD), jnp.float32))
        sums, outs = lax.scan(one_span, init, jnp.arange(N_SEQ, dtype=jnp.int32))
        q_all.append(outs[0].reshape(N_SEQ * SPAN, QH * HD))
        k_all.append(outs[1].reshape(N_SEQ * SPAN, KVH * HD))
        v_all.append(outs[2].reshape(N_SEQ * SPAN, KVH * HD))
        bk = sums[0].reshape(total, KVH * HD).astype(jnp.bfloat16)
        bv = sums[1].reshape(total, KVH * HD).astype(jnp.bfloat16)
        bk_all.append(bk)
        bv_all.append(bv)
        weight_grad = weight_grad + jnp.dot(beacon_hidden[doc].T, bk, preferred_element_type=jnp.float32)
    return (jnp.stack(q_all), jnp.stack(k_all), jnp.stack(v_all), jnp.stack(bk_all), jnp.stack(bv_all), weight_grad)
```

```python
import functools
import math

import jax
import jax.numpy as jnp
from jax import lax
from jax.experimental import pallas as pl
from jax.experimental.pallas import tpu as pltpu
from jax.sharding import Mesh
from jax.sharding import PartitionSpec as P

QH = 14
KVH = 2
HD = 128
GROUPS = QH // KVH
NEG = -1e30
SCALE = 1.0 / math.sqrt(HD)
LOG2E = math.log2(math.e)
CORES = 2
F32 = jnp.float32
BF16 = jnp.bfloat16


def grid_of(mesh):
    devices = mesh.devices
    dp, seq = devices.shape
    nx = 4 if seq == 128 else 2
    return dp, nx, seq // (nx * CORES)


def visible_bias(order_row, ratio_row, mine, core, nx, nz, slots, span):
    nseq = order_row.shape[1]
    t = lax.broadcasted_iota(jnp.int32, (nseq, nseq), 0)
    picks = jnp.where(order_row == t, 1.0, 0.0).astype(F32)
    rates = jnp.broadcast_to(ratio_row.astype(F32), (8, nseq))
    rate = jnp.dot(rates, picks, preferred_element_type=F32)[:1]
    cost = jnp.where(order_row < mine, rate, 4.0 * span)
    count = nx * nz * slots
    row = lax.broadcasted_iota(jnp.int32, (count, nseq), 0)
    lane = lax.broadcasted_iota(jnp.int32, (count, nseq), 1)
    owner = (row // slots) * CORES + core
    own_cost = jnp.sum(jnp.where(owner == lane, cost, 0.0), axis=1, keepdims=True)
    slot = lax.broadcasted_iota(jnp.int32, (count, 1), 0) % slots
    return jnp.where((slot + 1).astype(F32) * own_cost <= float(span), 0.0, NEG)


def attention_kernel(
    nx, nz, slots, span,
    place, order_s, order_row, ratio_row, q, up, k, v, near_k, near_v, far_k, far_v,
    dq, dk, dv, keep, send,
    bias, kcat, vcat, qcat, ucat, probs, dscores,
):
    half = nx * nz * slots
    per_x = nz * slots
    core = place[2]
    me = (place[0] * nz + place[1]) * CORES + core

    @pl.when(pl.program_id(0) == 0)
    def _():
        mine = order_s[me]
        args = (order_row[...], ratio_row[...], mine)
        near = visible_bias(*args, core, nx, nz, slots, span)
        far = visible_bias(*args, 1 - core, nx, nz, slots, span)
        bias[0:half, :] = jnp.broadcast_to(near, (half, HD))
        bias[half : 2 * half, :] = jnp.broadcast_to(far, (half, HD))

    kcat[0:span, :] = k[...]
    vcat[0:span, :] = v[...]
    for i in range(nx):
        lo = span + i * per_x
        kcat[lo : lo + per_x, :] = near_k[i, 0:per_x, :]
        vcat[lo : lo + per_x, :] = near_v[i, 0:per_x, :]
        lo += half
        kcat[lo : lo + per_x, :] = far_k[i, 0:per_x, :]
        vcat[lo : lo + per_x, :] = far_v[i, 0:per_x, :]
    for h in range(GROUPS):
        qcat[h * span : (h + 1) * span, :] = q[:, h * HD : (h + 1) * HD]
        ucat[h * span : (h + 1) * span, :] = up[:, h * HD : (h + 1) * HD]

    key_row = lax.broadcasted_iota(jnp.int32, (span, span), 0)
    query_col = lax.broadcasted_iota(jnp.int32, (span, span), 1)
    causal = key_row <= query_col
    contract_last = (((1,), (1,)), ((), ()))
    for h in range(GROUPS):
        rows = slice(h * span, (h + 1) * span)
        s = lax.dot_general(kcat[...], qcat[rows, :], contract_last, preferred_element_type=F32)
        dp = lax.dot_general(vcat[...], ucat[rows, :], contract_last, preferred_element_type=F32)
        s = s * (SCALE * LOG2E)
        s = jnp.concatenate(
            [jnp.where(causal, s[0:span, :], NEG), s[span:, :] + bias[...]], axis=0
        )
        top = jnp.max(s, axis=0, keepdims=True)
        e = jnp.exp2(s - top)
        inv = 1.0 / jnp.sum(e, axis=0, keepdims=True)
        delta = jnp.sum(e * dp, axis=0, keepdims=True) * inv
        p = e * inv
        probs[:, rows] = p.astype(BF16)
        dscores[:, rows] = (p * (dp - delta)).astype(BF16)

    full_k = (
        lax.dot_general(
            dscores[...], qcat[...], (((1,), (0,)), ((), ())), preferred_element_type=F32
        )
        * SCALE
    )
    full_v = lax.dot_general(
        probs[...], ucat[...], (((1,), (0,)), ((), ())), preferred_element_type=F32
    )
    dk[...] = full_k[0:span, :].astype(BF16)
    dv[...] = full_v[0:span, :].astype(BF16)
    keep[0] = full_k[span : span + half, :]
    keep[1] = full_v[span : span + half, :]
    send[0] = full_k[span + half :, :].astype(BF16)
    send[1] = full_v[span + half :, :].astype(BF16)
    dqt = (
        lax.dot_general(
            kcat[...], dscores[...], (((0,), (0,)), ((), ())), preferred_element_type=F32
        )
        * SCALE
    )
    for h in range(GROUPS):
        dq[:, h * HD : (h + 1) * HD] = dqt[:, h * span : (h + 1) * span].T.astype(BF16)


def attention(place, order, ratio, q, up, k, v, near, far, nx, nz, slots):
    span = q.shape[0]
    half = nx * nz * slots
    nseq = order.shape[0]
    rows = near.shape[1]
    keys = span + 2 * half
    smem = pl.BlockSpec(memory_space=pltpu.SMEM)
    row_spec = pl.BlockSpec((1, nseq), lambda g: (0, 0))
    wide = pl.BlockSpec((span, GROUPS * HD), lambda g: (0, g))
    slim = pl.BlockSpec((span, HD), lambda g: (0, g))
    beacon_k = pl.BlockSpec((nx, rows, HD), lambda g: (0, 0, g))
    beacon_v = pl.BlockSpec((nx, rows, HD), lambda g: (0, 0, KVH + g))
    part = pl.BlockSpec((2, half, HD), lambda g: (0, 0, g))
    flops = 5 * 2 * QH * span * keys * HD
    return pl.pallas_call(
        functools.partial(attention_kernel, nx, nz, slots, span),
        grid=(KVH,),
        in_specs=[
            smem, smem, row_spec, row_spec, wide, wide, slim, slim,
            beacon_k, beacon_v, beacon_k, beacon_v,
        ],
        out_specs=[wide, slim, slim, part, part],
        out_shape=[
            jax.ShapeDtypeStruct((span, QH * HD), BF16),
            jax.ShapeDtypeStruct((span, KVH * HD), BF16),
            jax.ShapeDtypeStruct((span, KVH * HD), BF16),
            jax.ShapeDtypeStruct((2, half, KVH * HD), F32),
            jax.ShapeDtypeStruct((2, half, KVH * HD), BF16),
        ],
        scratch_shapes=[
            pltpu.VMEM((2 * half, HD), F32),
            pltpu.VMEM((keys, HD), BF16),
            pltpu.VMEM((keys, HD), BF16),
            pltpu.VMEM((GROUPS * span, HD), BF16),
            pltpu.VMEM((GROUPS * span, HD), BF16),
            pltpu.VMEM((keys, GROUPS * span), BF16),
            pltpu.VMEM((keys, GROUPS * span), BF16),
        ],
        compiler_params=pltpu.CompilerParams(vmem_limit_bytes=48 * 1024 * 1024),
        cost_estimate=pl.CostEstimate(
            flops=flops, bytes_accessed=4 * 1024 * 1024, transcendentals=QH * span * keys
        ),
        name="attention",
    )(
        place, order, order.reshape(1, nseq), ratio.reshape(1, nseq),
        q, up, k, v, near, near, far, far,
    )


def spread_kernel(nx, per_x, keep, got, out):
    total_k = (keep[0] + got[0].astype(F32)).astype(BF16)
    total_v = (keep[1] + got[1].astype(F32)).astype(BF16)
    half = nx * per_x
    for i in range(nx):
        out[i, 0:half, :] = total_k
        out[i, half : half + per_x, :] = total_v[i * per_x : (i + 1) * per_x, :]


def spread(keep, got, nx):
    _, half, width = keep.shape
    per_x = half // nx
    return pl.pallas_call(
        functools.partial(spread_kernel, nx, per_x),
        out_shape=jax.ShapeDtypeStruct((nx, half + per_x, width), BF16),
        compiler_params=pltpu.CompilerParams(vmem_limit_bytes=32 * 1024 * 1024),
        cost_estimate=pl.CostEstimate(flops=0, bytes_accessed=4 * 1024 * 1024, transcendentals=0),
        name="spread",
    )(keep, got)


def weight_kernel(nx, nz, slots, ndp, rows_out, place, got, hidden, terms, weights, total):
    per_x = nz * slots
    half = nx * per_x
    width = got.shape[2]
    key_sum = got[0, 0:half, :].astype(F32)
    value_sum = got[0, half : half + per_x, :].astype(F32)
    for i in range(1, nx):
        key_sum = key_sum + got[i, 0:half, :].astype(F32)
        value_sum = value_sum + got[i, half : half + per_x, :].astype(F32)
    total[...] = key_sum
    mine = total[pl.ds(pl.multiple_of(place[0] * per_x, per_x), per_x), :]
    terms[:, 0:width] = mine.astype(BF16)
    terms[:, width:] = value_sum.astype(BF16)
    ordered = jnp.concatenate(
        [
            total[x * per_x + z * slots : x * per_x + (z + 1) * slots, :]
            for z in range(nz)
            for x in range(nx)
        ],
        axis=0,
    ).astype(BF16)
    parts = hidden.shape[1]
    lanes = hidden.shape[3]
    products = [
        lax.dot_general(
            hidden[:, part].reshape(half, lanes),
            ordered,
            (((0,), (0,)), ((), ())),
            preferred_element_type=F32,
        )
        for part in range(parts)
    ]
    product = jnp.concatenate(products, axis=0).astype(BF16)
    count = ndp * CORES * nz * 8
    row = lax.broadcasted_iota(jnp.int32, (count, parts * lanes), 0)
    column = lax.broadcasted_iota(jnp.int32, (count, parts * lanes), 1)
    item = row % 8
    z = (row // 8) % nz
    core = (row // (8 * nz)) % CORES
    y = row // (8 * nz * CORES)
    source = ((y * nz + z) * CORES + core) * rows_out + item
    picks = jnp.where((source == column) & (item < rows_out), 1.0, 0.0).astype(BF16)
    weights[...] = jnp.dot(picks, product, preferred_element_type=F32).astype(BF16)


def weight_terms(place, got, hidden, nx, nz, slots, ndp, rows_out):
    per_x = nz * slots
    width = got.shape[2]
    count = ndp * CORES * nz * 8
    vmem = pl.BlockSpec(memory_space=pltpu.VMEM)
    return pl.pallas_call(
        functools.partial(weight_kernel, nx, nz, slots, ndp, rows_out),
        in_specs=[pl.BlockSpec(memory_space=pltpu.SMEM), vmem, vmem],
        out_specs=[vmem, vmem],
        out_shape=[
            jax.ShapeDtypeStruct((per_x, 2 * width), BF16),
            jax.ShapeDtypeStruct((count, width), BF16),
        ],
        scratch_shapes=[pltpu.VMEM((nx * per_x, width), F32)],
        compiler_params=pltpu.CompilerParams(vmem_limit_bytes=48 * 1024 * 1024),
        cost_estimate=pl.CostEstimate(
            flops=2 * count * nx * per_x * width * 3,
            bytes_accessed=4 * 1024 * 1024,
            transcendentals=0,
        ),
        name="weight_terms",
    )(place, got, hidden)


def join_kernel(terms, weights, out):
    width = weights.shape[2]
    total = weights[0].astype(F32)
    for i in range(1, weights.shape[0]):
        total = total + weights[i].astype(F32)
    out[:, 0 : 2 * width] = terms[...]
    out[:, 2 * width :] = total.astype(BF16)


def join(terms, weights):
    rows, width = terms.shape
    return pl.pallas_call(
        join_kernel,
        out_shape=jax.ShapeDtypeStruct((rows, width + weights.shape[2]), BF16),
        cost_estimate=pl.CostEstimate(flops=0, bytes_accessed=1024 * 1024, transcendentals=0),
        name="join",
    )(terms, weights)


def per_device(
    nx, nz,
    queries, keys, values, grad_out, beacon_keys, beacon_values, beacon_hidden, order, ratio,
):
    ndp = lax.axis_size("dp")
    span = queries.shape[1]
    slots, width = beacon_keys.shape[1:]
    model = beacon_hidden.shape[2]
    rows_out = model // (ndp * nx * nz * CORES)
    place = jnp.stack([lax.axis_index("x"), lax.axis_index("z"), lax.axis_index("core")])
    place = place.astype(jnp.int32)

    mine = jnp.concatenate([beacon_keys[0], beacon_values[0]], axis=1)
    over_z = lax.all_to_all(
        jnp.broadcast_to(mine[None], (nz, slots, 2 * width)), "z", 0, 0, tiled=True
    )
    columns = model // nx
    padded = -(-columns // (2 * width)) * (2 * width)
    parts = padded // (2 * width)
    hidden = beacon_hidden[0].reshape(slots, ndp, nx, model // (ndp * nx))
    hidden = hidden.transpose(2, 0, 1, 3).reshape(nx, slots, columns)
    hidden = jnp.pad(hidden, ((0, 0), (0, 0), (0, padded - columns)))
    hidden = hidden.reshape(nx, slots, parts, 2 * width).transpose(0, 2, 1, 3)
    hidden = hidden.reshape(nx, parts * slots, 2 * width)
    message = jnp.concatenate(
        [jnp.broadcast_to(over_z.reshape(1, nz * slots, 2 * width), (nx, nz * slots, 2 * width)), hidden],
        axis=1,
    )
    near = lax.all_to_all(message, "x", 0, 0, tiled=True)
    far = lax.ppermute(near, "core", [(0, 1), (1, 0)])
    hidden = near[:, nz * slots :].reshape(nx, parts, slots, 2 * width)
    hidden = hidden.transpose(1, 0, 2, 3).reshape(1, parts, nx * slots, 2 * width)
    hidden = lax.all_gather(hidden, "z", axis=0, tiled=True)

    dq, dk, dv, keep, send = attention(
        place, order, ratio, queries[0], grad_out[0], keys[0], values[0], near, far, nx, nz, slots
    )

    got = lax.ppermute(send, "core", [(0, 1), (1, 0)])
    got = lax.all_to_all(spread(keep, got, nx), "x", 0, 0, tiled=True)
    terms, weights = weight_terms(place, got, hidden, nx, nz, slots, ndp, rows_out)
    weights = weights.reshape(ndp * CORES, nz * 8, width)
    weights = lax.all_to_all(weights, ("dp", "core"), 0, 0, tiled=True)
    last = join(terms, weights).reshape(nz, 8, 3 * width)
    last = lax.all_to_all(last, "z", 0, 0, tiled=True)
    sums = jnp.sum(last.astype(F32), axis=0)
    beacon_dk = sums[:slots, :width].astype(BF16)
    beacon_dv = sums[:slots, width : 2 * width].astype(BF16)
    weight_grad = sums[:rows_out, 2 * width :]
    return (dq[None], dk[None], dv[None], beacon_dk[None], beacon_dv[None], weight_grad)


def solution(mesh):
    ndp, nx, nz = grid_of(mesh)
    fine = Mesh(mesh.devices.reshape(ndp, nx, nz, CORES), ("dp", "x", "z", "core"))
    seq = ("x", "z", "core")
    split = P("dp", seq, None)
    return jax.shard_map(
        functools.partial(per_device, nx, nz),
        mesh=fine,
        in_specs=(split,) * 7 + (P(), P()),
        out_specs=(split,) * 5 + (P(("dp",) + seq, None),),
        check_vma=False,
    )
```

```python
import functools
import math

import jax
import jax.numpy as jnp
from jax import lax
from jax.experimental import pallas as pl
from jax.experimental.pallas import tpu as pltpu
from jax.sharding import Mesh
from jax.sharding import PartitionSpec as P

QH = 14
KVH = 2
HD = 128
GROUPS = QH // KVH
NEG = -1e30
SCALE = 1.0 / math.sqrt(HD)
LOG2E = math.log2(math.e)
CORES = 2
SUB = 8
F32 = jnp.float32
BF16 = jnp.bfloat16


def grid_of(mesh):
    dp, seq = mesh.devices.shape
    nx, nzl = (4, 4) if seq == 128 else (2, 2)
    return dp, nx, seq // (nx * nzl * CORES), nzl


def visible_bias(order_row, ratio_row, mine, core, nx, nz, slots, span):
    nseq = order_row.shape[1]
    t = lax.broadcasted_iota(jnp.int32, (nseq, nseq), 0)
    picks = jnp.where(order_row == t, 1.0, 0.0).astype(F32)
    rates = jnp.broadcast_to(ratio_row.astype(F32), (8, nseq))
    rate = jnp.dot(rates, picks, preferred_element_type=F32)[:1]
    cost = jnp.where(order_row < mine, rate, 4.0 * span)
    count = nx * nz * slots
    row = lax.broadcasted_iota(jnp.int32, (count, nseq), 0)
    lane = lax.broadcasted_iota(jnp.int32, (count, nseq), 1)
    owner = (row // slots) * CORES + core
    own_cost = jnp.sum(jnp.where(owner == lane, cost, 0.0), axis=1, keepdims=True)
    slot = lax.broadcasted_iota(jnp.int32, (count, 1), 0) % slots
    return jnp.where((slot + 1).astype(F32) * own_cost <= float(span), 0.0, NEG)


def attention_kernel(
    nx, nzh, nzl, slots, span,
    place, order_s, order_row, ratio_row, q, up, k, v, near_k, near_v, far_k, far_v,
    dq, dk, dv, keep, send,
    bias, kcat, vcat, qcat, ucat, probs, dscores,
):
    nz = nzh * nzl
    half = nx * nz * slots
    core = place[2]
    me = (place[0] * nz + place[1]) * CORES + core

    @pl.when(pl.program_id(0) == 0)
    def _():
        mine = order_s[me]
        args = (order_row[...], ratio_row[...], mine)
        near = visible_bias(*args, core, nx, nz, slots, span)
        far = visible_bias(*args, 1 - core, nx, nz, slots, span)
        bias[0:half, :] = jnp.broadcast_to(near, (half, HD))
        bias[half : 2 * half, :] = jnp.broadcast_to(far, (half, HD))

    for cat, own, near, far in ((kcat, k, near_k, far_k), (vcat, v, near_v, far_v)):
        cat[0:span, :] = own[...]
        cat[span : span + half, :] = near[...]
        cat[span + half :, :] = far[...]
    for h in range(GROUPS):
        qcat[h * span : (h + 1) * span, :] = q[:, h * HD : (h + 1) * HD]
        ucat[h * span : (h + 1) * span, :] = up[:, h * HD : (h + 1) * HD]

    key_row = lax.broadcasted_iota(jnp.int32, (span, span), 0)
    query_col = lax.broadcasted_iota(jnp.int32, (span, span), 1)
    causal = key_row <= query_col
    contract_last = (((1,), (1,)), ((), ()))
    for h in range(GROUPS):
        rows = slice(h * span, (h + 1) * span)
        s = lax.dot_general(kcat[...], qcat[rows, :], contract_last, preferred_element_type=F32)
        dp = lax.dot_general(vcat[...], ucat[rows, :], contract_last, preferred_element_type=F32)
        s = s * (SCALE * LOG2E)
        s = jnp.concatenate(
            [jnp.where(causal, s[0:span, :], NEG), s[span:, :] + bias[...]], axis=0
        )
        top = jnp.max(s, axis=0, keepdims=True)
        e = jnp.exp2(s - top)
        inv = 1.0 / jnp.sum(e, axis=0, keepdims=True)
        delta = jnp.sum(e * dp, axis=0, keepdims=True) * inv
        p = e * inv
        probs[:, rows] = p.astype(BF16)
        dscores[:, rows] = (p * (dp - delta)).astype(BF16)

    full_k = (
        lax.dot_general(
            dscores[...], qcat[...], (((1,), (0,)), ((), ())), preferred_element_type=F32
        )
        * SCALE
    )
    full_v = lax.dot_general(
        probs[...], ucat[...], (((1,), (0,)), ((), ())), preferred_element_type=F32
    )
    dk[...] = full_k[0:span, :].astype(BF16)
    dv[...] = full_v[0:span, :].astype(BF16)
    for kind, full in ((0, full_k), (1, full_v)):
        for out, lo in ((keep, span), (send, span + half)):
            rows = full[lo : lo + half, :].reshape(nx, nzh, nzl, slots, HD)
            out[kind] = jnp.swapaxes(rows, 1, 2).reshape(half, HD).astype(out.dtype)
    dqt = (
        lax.dot_general(
            kcat[...], dscores[...], (((0,), (0,)), ((), ())), preferred_element_type=F32
        )
        * SCALE
    )
    for h in range(GROUPS):
        dq[:, h * HD : (h + 1) * HD] = dqt[:, h * span : (h + 1) * span].T.astype(BF16)


def attention(place, order, ratio, q, up, k, v, near, far, nx, nzh, nzl, slots):
    span = q.shape[0]
    half = nx * nzh * nzl * slots
    nseq = order.shape[0]
    keys = span + 2 * half
    row_spec = pl.BlockSpec((1, nseq), lambda g: (0, 0))
    wide = pl.BlockSpec((span, GROUPS * HD), lambda g: (0, g))
    slim = pl.BlockSpec((span, HD), lambda g: (0, g))
    beacon_k = pl.BlockSpec((half, HD), lambda g: (0, g))
    beacon_v = pl.BlockSpec((half, HD), lambda g: (0, KVH + g))
    part = pl.BlockSpec((2, half, HD), lambda g: (0, 0, g))
    flops = 5 * 2 * QH * span * keys * HD
    return pl.pallas_call(
        functools.partial(attention_kernel, nx, nzh, nzl, slots, span),
        grid=(KVH,),
        in_specs=[
            SMEM, SMEM, row_spec, row_spec, wide, wide, slim, slim,
            beacon_k, beacon_v, beacon_k, beacon_v,
        ],
        out_specs=[wide, slim, slim, part, part],
        out_shape=[
            jax.ShapeDtypeStruct((span, QH * HD), BF16),
            jax.ShapeDtypeStruct((span, KVH * HD), BF16),
            jax.ShapeDtypeStruct((span, KVH * HD), BF16),
            jax.ShapeDtypeStruct((2, half, KVH * HD), F32),
            jax.ShapeDtypeStruct((2, half, KVH * HD), BF16),
        ],
        scratch_shapes=[
            pltpu.VMEM((2 * half, HD), F32),
            pltpu.VMEM((keys, HD), BF16),
            pltpu.VMEM((keys, HD), BF16),
            pltpu.VMEM((GROUPS * span, HD), BF16),
            pltpu.VMEM((GROUPS * span, HD), BF16),
            pltpu.VMEM((keys, GROUPS * span), BF16),
            pltpu.VMEM((keys, GROUPS * span), BF16),
        ],
        compiler_params=pltpu.CompilerParams(vmem_limit_bytes=48 * 1024 * 1024),
        cost_estimate=pl.CostEstimate(
            flops=flops, bytes_accessed=4 * 1024 * 1024, transcendentals=QH * span * keys
        ),
        name="attention",
    )(
        place, order, order.reshape(1, nseq), ratio.reshape(1, nseq),
        q, up, k, v, near, near, far, far,
    )


def add_blocks(ref):
    total = ref[0].astype(F32)
    for i in range(1, ref.shape[0]):
        total = total + ref[i].astype(F32)
    return total


VMEM = pl.BlockSpec(memory_space=pltpu.VMEM)
SMEM = pl.BlockSpec(memory_space=pltpu.SMEM)


def small_call(kernel, name, outs, *args, flops=0, scratch=()):
    size = sum(a.size * a.dtype.itemsize for a in args)
    size += sum(o.size * jnp.dtype(o.dtype).itemsize for o in outs)
    return pl.pallas_call(
        kernel,
        in_specs=[SMEM if a.dtype == jnp.int32 else VMEM for a in args],
        out_specs=[VMEM for _ in outs],
        out_shape=outs,
        scratch_shapes=list(scratch),
        compiler_params=pltpu.CompilerParams(vmem_limit_bytes=32 * 1024 * 1024),
        cost_estimate=pl.CostEstimate(flops=flops, bytes_accessed=size, transcendentals=0),
        name=name,
    )(*args)


def bf16(*shape):
    return jax.ShapeDtypeStruct(shape, BF16)


def message_kernel(groups, nz, rows_out, keys, values, hidden, out):
    slots, width = keys.shape
    chunk = hidden.shape[1] // groups
    pieces = [hidden[:, i * chunk : (i + 1) * chunk].astype(F32) for i in range(groups)]
    if groups * slots < HD:
        pieces.append(jnp.zeros((HD - groups * slots, chunk), F32))
    stacked = jnp.concatenate(pieces, axis=0).astype(BF16)
    row = lax.broadcasted_iota(jnp.int32, (nz * CORES * SUB, chunk), 0)
    column = lax.broadcasted_iota(jnp.int32, (nz * CORES * SUB, chunk), 1)
    item = row % SUB
    picks = (column == (row // SUB) * rows_out + item) & (item < rows_out)
    turned = lax.dot_general(
        jnp.where(picks, 1.0, 0.0).astype(BF16),
        stacked,
        (((1,), (1,)), ((), ())),
        preferred_element_type=F32,
    ).reshape(nz, CORES, SUB, HD)
    out[:, 0:width] = jnp.concatenate([keys[...].astype(F32)] * nz, axis=0).astype(BF16)
    out[:, width : 2 * width] = jnp.concatenate([values[...].astype(F32)] * nz, axis=0).astype(BF16)
    for core in range(CORES):
        lo = 2 * width + core * HD
        out[:, lo : lo + HD] = turned[:, core].reshape(nz * SUB, HD).astype(BF16)


def message(keys, values, hidden, groups, nz, rows_out):
    slots, width = keys.shape
    return small_call(
        functools.partial(message_kernel, groups, nz, rows_out), "message",
        [bf16(nz * slots, 2 * width + CORES * HD)], keys, values, hidden,
    )[0]


def turn_kernel(groups, nzh, nzl, got, out):
    count = groups * CORES * SUB
    lanes = CORES * HD
    slots = SUB
    row = lax.broadcasted_iota(jnp.int32, (count, lanes), 0)
    lane = lax.broadcasted_iota(jnp.int32, (count, lanes), 1)
    mine = ((lane // HD) == (row // SUB) % CORES) & (((lane % HD) // slots) == row // (SUB * CORES))
    from_lane = lax.broadcasted_iota(jnp.int32, (lanes, nzh * nzl * slots), 0)
    to_lane = lax.broadcasted_iota(jnp.int32, (lanes, nzh * nzl * slots), 1)
    total = jnp.zeros((count, nzh * nzl * slots), F32)
    for zh in range(nzh):
        for zl in range(nzl):
            z = zh * nzl + zl
            block = got[z * SUB : (z + 1) * SUB, :].astype(F32)
            block = jnp.where(mine, jnp.concatenate([block] * (count // SUB), axis=0), 0.0)
            place = to_lane == (zl * nzh + zh) * slots + from_lane % slots
            total = total + jnp.dot(
                block.astype(BF16),
                jnp.where(place, 1.0, 0.0).astype(BF16),
                preferred_element_type=F32,
            )
    out[...] = total.astype(BF16)


def turn(got, groups, nzh, nzl):
    shape = bf16(groups * CORES * SUB, nzh * nzl * SUB)
    return small_call(functools.partial(turn_kernel, groups, nzh, nzl), "turn", [shape], got)[0]


def merge_kernel(keep, got, out):
    width = keep.shape[2]
    out[:, 0:width] = (keep[0] + got[0].astype(F32)).astype(BF16)
    out[:, width:] = (keep[1] + got[1].astype(F32)).astype(BF16)


def merge(keep, got):
    _, rows, width = keep.shape
    return small_call(merge_kernel, "merge", [bf16(rows, 2 * width)], keep, got)[0]


def zh_kernel(slots, got, out):
    total = add_blocks(got)
    rows = total.shape[0]
    width = total.shape[1] // 2
    keys = total[:, 0:width].astype(BF16)
    for zh in range(out.shape[0]):
        own = total[zh * slots : (zh + 1) * slots, width:]
        out[zh, 0:rows, :] = keys
        out[zh, rows:, :] = jnp.concatenate([own, jnp.zeros_like(own)], axis=0).astype(BF16)


def zh_message(got, nzh, slots):
    _, rows, lanes = got.shape
    shape = bf16(nzh, rows + 2 * slots, lanes // 2)
    return small_call(functools.partial(zh_kernel, slots), "zh_message", [shape], got)[0]


def owner_kernel(slots, rows, place, got, keys, values, spread, total):
    total[...] = add_blocks(got)
    first = pl.multiple_of(place[1] * slots, slots)
    keys[...] = total[pl.ds(first, slots), :].astype(BF16)
    values[...] = total[rows : rows + slots, :].astype(BF16)
    every = total[0:rows, :].astype(BF16)
    for zl in range(spread.shape[0]):
        spread[zl] = every


def owner_rows(place, got, nzl, slots):
    nzh, tall, width = got.shape
    rows = nzh * slots
    return small_call(
        functools.partial(owner_kernel, slots, rows), "owner_rows",
        [bf16(slots, width), bf16(slots, width), bf16(nzl, rows, width)], place, got,
        scratch=[pltpu.VMEM((tall, width), F32)],
    )


def weight_kernel(hidden, keys, out):
    out[...] = jnp.dot(hidden[...], keys[...], preferred_element_type=F32).astype(BF16)


def weight_terms(hidden, keys):
    rows, width = keys.shape
    count = hidden.shape[0]
    return small_call(
        weight_kernel, "weight_terms", [bf16(count, width)], hidden, keys,
        flops=2 * count * rows * width,
    )[0]


def per_device(
    nx, nzh, nzl,
    queries, keys, values, grad_out, beacon_keys, beacon_values, beacon_hidden, order, ratio,
):
    ndp = lax.axis_size("dp")
    nz = nzh * nzl
    slots, width = beacon_keys.shape[1:]
    model = beacon_hidden.shape[2]
    groups = ndp * nx
    rows_out = model // (groups * nz * CORES)
    half = nx * nz * slots
    swap = [(0, 1), (1, 0)]
    zh, zl = lax.axis_index("zh"), lax.axis_index("zl")
    place = [lax.axis_index("x"), zh * nzl + zl, lax.axis_index("core")]
    place = jnp.stack(place).astype(jnp.int32)
    zh_place = jnp.stack([zl, zh]).astype(jnp.int32)

    first = message(beacon_keys[0], beacon_values[0], beacon_hidden[0], groups, nz, rows_out)
    first = lax.all_to_all(first.reshape(nz, slots, -1), ("zh", "zl"), 0, 0, tiled=True)
    near = first[:, :, : 2 * width].reshape(1, nz * slots, 2 * width)
    near = jnp.broadcast_to(near, (nx, nz * slots, 2 * width))
    near = lax.all_to_all(near, "x", 0, 0, tiled=True).reshape(half, 2 * width)
    far = lax.ppermute(near, "core", swap)
    hidden = turn(first[:, :, 2 * width :].reshape(nz * slots, CORES * HD), groups, nzh, nzl)

    dq, dk, dv, keep, send = attention(
        place, order, ratio, queries[0], grad_out[0], keys[0], values[0], near, far,
        nx, nzh, nzl, slots,
    )

    terms = merge(keep, lax.ppermute(send, "core", swap))
    terms = terms.reshape(nx * nzl, nzh * slots, 2 * width)
    terms = lax.all_to_all(terms, ("x", "zl"), 0, 0, tiled=True)
    terms = lax.all_to_all(zh_message(terms, nzh, slots), "zh", 0, 0, tiled=True)
    beacon_dk, beacon_dv, spread = owner_rows(zh_place, terms, nzl, slots)
    spread = lax.all_to_all(spread, "zl", 0, 0, tiled=True).reshape(nz * slots, width)
    weights = weight_terms(hidden, spread).reshape(groups * CORES, SUB, width)
    weights = lax.all_to_all(weights, ("dp", "x", "core"), 0, 0, tiled=True)
    weight_grad = jnp.sum(weights.astype(F32), axis=0)[:rows_out]
    return (dq[None], dk[None], dv[None], beacon_dk[None], beacon_dv[None], weight_grad)


def solution(mesh):
    ndp, nx, nzh, nzl = grid_of(mesh)
    fine = Mesh(
        mesh.devices.reshape(ndp, nx, nzh, nzl, CORES), ("dp", "x", "zh", "zl", "core")
    )
    seq = ("x", "zh", "zl", "core")
    split = P("dp", seq, None)
    return jax.shard_map(
        functools.partial(per_device, nx, nzh, nzl),
        mesh=fine,
        in_specs=(split,) * 7 + (P(), P()),
        out_specs=(split,) * 5 + (P(("dp",) + seq, None),),
        check_vma=False,
    )
```

```python
import functools
import math

import jax
import jax.numpy as jnp
from jax import lax
from jax.experimental import pallas as pl
from jax.experimental.pallas import tpu as pltpu
from jax.sharding import Mesh
from jax.sharding import PartitionSpec as P

QH = 14
KVH = 2
HD = 128
GROUPS = QH // KVH
NEG = -1e30
SCALE = 1.0 / math.sqrt(HD)
LOG2E = math.log2(math.e)
CORES = 2
SUB = 8
HEADS = 4
F32 = jnp.float32
BF16 = jnp.bfloat16


def grid_of(mesh):
    dp, seq = mesh.devices.shape
    nx, nzl = (4, 4) if seq == 128 else (2, 2)
    return dp, nx, seq // (nx * nzl * CORES), nzl


def visible_bias(order_row, ratio_row, mine, slots, span):
    nseq = order_row.shape[1]
    t = lax.broadcasted_iota(jnp.int32, (nseq, nseq), 0)
    picks = jnp.where(order_row == t, 1.0, 0.0).astype(F32)
    rates = jnp.broadcast_to(ratio_row.astype(F32), (slots, nseq))
    rate = jnp.dot(rates, picks, preferred_element_type=F32)
    cost = jnp.where(order_row < mine, rate, 4.0 * span)
    slot = lax.broadcasted_iota(jnp.int32, (slots, nseq), 0)
    return jnp.where((slot + 1).astype(F32) * cost <= float(span), 0.0, NEG)


def attention_kernel(
    nx, nzh, nzl, slots,
    bias, mine, other, beacons,
    own_out, other_out, terms,
    kcat, vcat, qcat, ucat, probs, dscores,
):
    span = mine.shape[0]
    wide = GROUPS * HD
    sides = (mine, other)
    for r, side in enumerate(sides):
        kcat[r, 0:span, :] = side[:, 2 * wide : 2 * wide + HD]
        vcat[r, 0:span, :] = side[:, 2 * wide + HD :]
        kcat[r, span:, :] = beacons[:, 0:HD]
        vcat[r, span:, :] = beacons[:, HD:]
        for h in range(GROUPS):
            at = (r * GROUPS + h) * span
            qcat[at : at + span, :] = side[:, h * HD : (h + 1) * HD]
            ucat[at : at + span, :] = side[:, wide + h * HD : wide + (h + 1) * HD]

    key_row = lax.broadcasted_iota(jnp.int32, (span, span), 0)
    query_col = lax.broadcasted_iota(jnp.int32, (span, span), 1)
    causal = key_row <= query_col
    contract_last = (((1,), (1,)), ((), ()))
    contract_first = (((0,), (0,)), ((), ()))

    for r in range(CORES):
        for h0 in range(0, GROUPS, HEADS):
            heads = min(HEADS, GROUPS - h0)
            lo = (r * GROUPS + h0) * span
            rows = slice(lo, lo + heads * span)
            s = lax.dot_general(
                kcat[r], qcat[rows, :], contract_last, preferred_element_type=F32
            )
            dp = lax.dot_general(
                vcat[r], ucat[rows, :], contract_last, preferred_element_type=F32
            )
            s = s * (SCALE * LOG2E)
            own = jnp.where(jnp.concatenate([causal] * heads, axis=1), s[0:span, :], NEG)
            far = s[span:, :] + jnp.concatenate([bias[r]] * heads, axis=1)
            s = jnp.concatenate([own, far], axis=0)
            top = jnp.max(s, axis=0, keepdims=True)
            e = jnp.exp2(s - top)
            inv = 1.0 / jnp.sum(e, axis=0, keepdims=True)
            delta = jnp.sum(e * dp, axis=0, keepdims=True) * inv
            p = e * inv
            probs[:, rows] = p.astype(BF16)
            dscores[:, rows] = (p * (dp - delta)).astype(BF16)

    products = ((0, dscores, qcat, SCALE), (1, probs, ucat, 1.0))
    for kind, left, right, scale in products:
        full = jnp.dot(left[span:, :], right[...], preferred_element_type=F32) * scale
        count = full.shape[0]
        full = full.reshape(nx, nzh, nzl, CORES * slots, HD)
        full = jnp.swapaxes(full, 1, 2).reshape(count, HD)
        terms[:, kind * HD : (kind + 1) * HD] = full.astype(BF16)
    for r, out in enumerate((own_out, other_out)):
        rows = slice(r * wide, (r + 1) * wide)
        for kind, left, right, scale in products:
            part = jnp.dot(left[0:span, rows], right[rows, :], preferred_element_type=F32)
            lo = wide + kind * HD
            out[:, lo : lo + HD] = (part * scale).astype(BF16)
        part = lax.dot_general(
            kcat[r], dscores[:, rows], contract_first, preferred_element_type=F32
        ) * SCALE
        for h in range(GROUPS):
            lanes = slice(h * HD, (h + 1) * HD)
            out[:, lanes] = part[:, h * span : (h + 1) * span].T.astype(BF16)


def attention(bias, mine, other, beacons, nx, nzh, nzl, slots):
    span = mine.shape[0]
    total, lanes = beacons.shape
    keys = span + total
    wide = GROUPS * HD
    return small_call(
        functools.partial(attention_kernel, nx, nzh, nzl, slots), "attention",
        [bf16(span, wide + lanes), bf16(span, wide + lanes), bf16(total, lanes)],
        bias, mine, other, beacons,
        flops=5 * 2 * QH * span * keys * HD,
        scratch=[
            pltpu.VMEM((CORES, keys, HD), BF16),
            pltpu.VMEM((CORES, keys, HD), BF16),
            pltpu.VMEM((CORES * wide, HD), BF16),
            pltpu.VMEM((CORES * wide, HD), BF16),
            pltpu.VMEM((keys, CORES * wide), BF16),
            pltpu.VMEM((keys, CORES * wide), BF16),
        ],
    )


def add_blocks(ref):
    total = ref[0].astype(F32)
    for i in range(1, ref.shape[0]):
        total = total + ref[i].astype(F32)
    return total


VMEM = pl.BlockSpec(memory_space=pltpu.VMEM)
SMEM = pl.BlockSpec(memory_space=pltpu.SMEM)


def small_call(kernel, name, outs, *args, flops=0, scratch=()):
    size = sum(a.size * a.dtype.itemsize for a in args)
    size += sum(o.size * jnp.dtype(o.dtype).itemsize for o in outs)
    return pl.pallas_call(
        kernel,
        in_specs=[SMEM if a.dtype == jnp.int32 else VMEM for a in args],
        out_specs=[VMEM for _ in outs],
        out_shape=outs,
        scratch_shapes=list(scratch),
        compiler_params=pltpu.CompilerParams(vmem_limit_bytes=48 * 1024 * 1024),
        cost_estimate=pl.CostEstimate(flops=flops, bytes_accessed=size, transcendentals=0),
        name=name,
    )(*args)


def bf16(*shape):
    return jax.ShapeDtypeStruct(shape, BF16)


def message_kernel(groups, nz, rows_out, keys_in, values_in, hidden_in, out, keys, values, hidden, sems):
    copies = [
        pltpu.make_async_copy(source, held, sems.at[i])
        for i, (source, held) in enumerate(
            ((hidden_in, hidden), (keys_in, keys), (values_in, values))
        )
    ]
    for copy in copies:
        copy.start()
    for copy in copies:
        copy.wait()
    slots, width = keys.shape
    chunk = hidden.shape[1] // groups
    pieces = [hidden[:, i * chunk : (i + 1) * chunk].astype(F32) for i in range(groups)]
    if groups * slots < HD:
        pieces.append(jnp.zeros((HD - groups * slots, chunk), F32))
    stacked = jnp.concatenate(pieces, axis=0).astype(BF16)
    row = lax.broadcasted_iota(jnp.int32, (nz * CORES * SUB, chunk), 0)
    column = lax.broadcasted_iota(jnp.int32, (nz * CORES * SUB, chunk), 1)
    item = row % SUB
    picks = (column == (row // SUB) * rows_out + item) & (item < rows_out)
    turned = lax.dot_general(
        jnp.where(picks, 1.0, 0.0).astype(BF16),
        stacked,
        (((1,), (1,)), ((), ())),
        preferred_element_type=F32,
    )
    both = []
    for core in range(CORES):
        lanes = slice(core * HD, (core + 1) * HD)
        both.append(jnp.concatenate([keys[:, lanes], values[:, lanes]], axis=1).astype(F32))
    out[:, 0:width] = jnp.concatenate(both * nz, axis=0).astype(BF16)
    out[:, width:] = turned.astype(BF16)


def message(keys, values, hidden, groups, nz, rows_out):
    slots, width = keys.shape
    anywhere = pl.BlockSpec(memory_space=pl.ANY)
    return pl.pallas_call(
        functools.partial(message_kernel, groups, nz, rows_out),
        in_specs=[anywhere] * 3,
        out_specs=VMEM,
        out_shape=bf16(nz * CORES * slots, width + HD),
        scratch_shapes=[
            *[pltpu.VMEM(a.shape, BF16) for a in (keys, values, hidden)],
            pltpu.SemaphoreType.DMA((3,)),
        ],
        compiler_params=pltpu.CompilerParams(vmem_limit_bytes=56 * 1024 * 1024),
        cost_estimate=pl.CostEstimate(
            flops=0, bytes_accessed=512 * 1024, transcendentals=0
        ),
        name="message",
    )(keys, values, hidden)


def split_kernel(place, q, up, k, v, mine, send):
    wide = GROUPS * HD
    core = place[2]
    for out, head in ((mine, core), (send, 1 - core)):
        lanes = pl.ds(pl.multiple_of(head * wide, HD), wide)
        out[:, 0:wide] = q[:, lanes]
        out[:, wide : 2 * wide] = up[:, lanes]
        lanes = pl.ds(pl.multiple_of(head * HD, HD), HD)
        out[:, 2 * wide : 2 * wide + HD] = k[:, lanes]
        out[:, 2 * wide + HD :] = v[:, lanes]


def split_heads(place, q, up, k, v):
    shape = bf16(q.shape[0], 2 * GROUPS * HD + 2 * HD)
    return small_call(split_kernel, "split_heads", [shape, shape], place, q, up, k, v)


def join_kernel(place, mine, got, dq, dk, dv):
    wide = GROUPS * HD
    core = place[2]
    for part, head in ((mine, core), (got, 1 - core)):
        dq[:, pl.ds(pl.multiple_of(head * wide, HD), wide)] = part[:, 0:wide]
        lanes = pl.ds(pl.multiple_of(head * HD, HD), HD)
        dk[:, lanes] = part[:, wide : wide + HD]
        dv[:, lanes] = part[:, wide + HD :]


def join_heads(place, mine, got):
    span = mine.shape[0]
    shapes = [bf16(span, QH * HD), bf16(span, KVH * HD), bf16(span, KVH * HD)]
    return small_call(join_kernel, "join_heads", shapes, place, mine, got)


def mask_kernel(nz, slots, span, place, order_s, order_row, ratio_row, bias):
    core = place[2]
    first = (place[0] * nz + place[1]) * CORES
    for r, index in enumerate((first + core, first + 1 - core)):
        owners = visible_bias(order_row[...], ratio_row[...], order_s[index], slots, span)
        for j in range(owners.shape[1]):
            tile = jnp.broadcast_to(owners[:, j : j + 1], (slots, HD))
            bias[r, j * slots : (j + 1) * slots, :] = tile


def mask(place, order, ratio, nz, slots, span):
    nseq = order.shape[0]
    return pl.pallas_call(
        functools.partial(mask_kernel, nz, slots, span),
        in_specs=[SMEM, SMEM, VMEM, VMEM],
        out_specs=VMEM,
        out_shape=jax.ShapeDtypeStruct((CORES, nseq * slots, HD), F32),
        compiler_params=pltpu.CompilerParams(vmem_limit_bytes=32 * 1024 * 1024),
        cost_estimate=pl.CostEstimate(
            flops=0, bytes_accessed=2 * 1024 * 1024, transcendentals=0
        ),
        name="mask",
    )(place, order, order.reshape(1, nseq), ratio.reshape(1, nseq))


def turn_kernel(groups, nzh, nzl, slots, got, out):
    count = groups * SUB
    width = nzh * nzl * CORES * slots
    row = lax.broadcasted_iota(jnp.int32, (count, HD), 0)
    lane = lax.broadcasted_iota(jnp.int32, (count, HD), 1)
    same = lane // slots == row // SUB
    from_lane = lax.broadcasted_iota(jnp.int32, (HD, width), 0)
    to_lane = lax.broadcasted_iota(jnp.int32, (HD, width), 1)
    total = jnp.zeros((count, width), F32)
    for zh in range(nzh):
        for zl in range(nzl):
            for c in range(CORES):
                source = (zh * nzl + zl) * CORES + c
                target = (zl * nzh + zh) * CORES + c
                block = got[source * SUB : (source + 1) * SUB, :].astype(F32)
                block = jnp.where(same, jnp.concatenate([block] * groups, axis=0), 0.0)
                put = to_lane == target * slots + from_lane % slots
                total = total + jnp.dot(
                    block.astype(BF16),
                    jnp.where(put, 1.0, 0.0).astype(BF16),
                    preferred_element_type=F32,
                )
    out[...] = total.astype(BF16)


def turn(got, groups, nzh, nzl, slots):
    shape = bf16(groups * SUB, nzh * nzl * CORES * slots)
    kernel = functools.partial(turn_kernel, groups, nzh, nzl, slots)
    return small_call(kernel, "turn", [shape], got)[0]


def zh_kernel(got, out):
    total = add_blocks(got)
    rows = total.shape[0]
    each = rows // out.shape[0]
    keys = total[:, 0:HD].astype(BF16)
    for zh in range(out.shape[0]):
        out[zh, 0:rows, :] = keys
        out[zh, rows:, :] = total[zh * each : (zh + 1) * each, HD:].astype(BF16)


def zh_message(got, nzh):
    _, rows, _ = got.shape
    return small_call(zh_kernel, "zh_message", [bf16(nzh, rows + rows // nzh, HD)], got)[0]


def spread_kernel(got, out):
    total = add_blocks(got).astype(BF16)
    for i in range(out.shape[0]):
        out[i] = total


def spread(got, peers):
    return small_call(spread_kernel, "spread", [bf16(peers, *got.shape[1:])], got)[0]


def weight_kernel(rows, hidden, got, out):
    pairs = []
    for zl in range(got.shape[0] // CORES):
        heads = [got[zl * CORES + c, 0:rows, :] for c in range(CORES)]
        pairs.append(jnp.concatenate(heads, axis=1))
    keys = jnp.concatenate(pairs, axis=0)
    out[...] = jnp.dot(hidden[...], keys, preferred_element_type=F32).astype(BF16)


def weight_terms(hidden, got, rows):
    count, depth = hidden.shape
    return small_call(
        functools.partial(weight_kernel, rows), "weight_terms", [bf16(count, CORES * HD)],
        hidden, got, flops=2 * count * depth * CORES * HD,
    )[0]


def finish_kernel(nzl, slots, rows, place, got, weights, keys, values, weight_grad, held):
    zh, zl = place[1] // nzl, place[1] % nzl
    core = place[2]
    key_row = pl.multiple_of((zh * CORES + core) * slots, slots)
    value_row = pl.multiple_of(rows + core * slots, slots)
    for c in range(CORES):
        held[c] = got[pl.ds(zl * CORES + c, 1)][0].astype(F32)
        lanes = slice(c * HD, (c + 1) * HD)
        keys[:, lanes] = held[c, pl.ds(key_row, slots), :].astype(BF16)
        values[:, lanes] = held[c, pl.ds(value_row, slots), :].astype(BF16)
    weight_grad[...] = add_blocks(weights)[0 : weight_grad.shape[0], :]


def finish(place, got, weights, nzl, slots, rows, rows_out):
    width = weights.shape[2]
    return small_call(
        functools.partial(finish_kernel, nzl, slots, rows), "finish",
        [
            bf16(slots, width),
            bf16(slots, width),
            jax.ShapeDtypeStruct((rows_out, width), F32),
        ],
        place, got, weights, scratch=[pltpu.VMEM((CORES, *got.shape[1:]), F32)],
    )


def per_device(
    nx, nzh, nzl,
    queries, keys, values, grad_out, beacon_keys, beacon_values, beacon_hidden, order, ratio,
):
    ndp = lax.axis_size("dp")
    nz = nzh * nzl
    span = queries.shape[1]
    slots, width = beacon_keys.shape[1:]
    model = beacon_hidden.shape[2]
    groups = ndp * nx
    rows_out = model // (groups * nz * CORES)
    swap = [(0, 1), (1, 0)]
    z_index = lax.axis_index("zh") * nzl + lax.axis_index("zl")
    place = jnp.stack([lax.axis_index("x"), z_index, lax.axis_index("core")]).astype(jnp.int32)

    first = message(beacon_keys[0], beacon_values[0], beacon_hidden[0], groups, nz, rows_out)
    first = first.reshape(nz * CORES, slots, width + HD)
    first = lax.all_to_all(first, ("zh", "zl", "core"), 0, 0, tiled=True)
    mine, send = split_heads(place, queries[0], grad_out[0], keys[0], values[0])
    other = lax.ppermute(send, "core", swap)
    bias = mask(place, order, ratio, nz, slots, span)
    first, mine, other, bias = lax.optimization_barrier((first, mine, other, bias))

    beacons = first[:, :, :width].reshape(1, nz * CORES * slots, width)
    beacons = jnp.broadcast_to(beacons, (nx, nz * CORES * slots, width))
    beacons = lax.all_to_all(beacons, "x", 0, 0, tiled=True)
    beacons = beacons.reshape(nx * nz * CORES * slots, width)

    own_out, other_out, terms = attention(bias, mine, other, beacons, nx, nzh, nzl, slots)

    terms = terms.reshape(nx * nzl, nzh * CORES * slots, width)
    terms = lax.all_to_all(terms, ("x", "zl"), 0, 0, tiled=True)
    dq, dk, dv = join_heads(place, own_out, lax.ppermute(other_out, "core", swap))
    hidden = first[:, :, width:].reshape(nz * CORES * slots, HD)
    hidden = turn(hidden, groups, nzh, nzl, slots)
    terms, hidden, dq, dk, dv = lax.optimization_barrier((terms, hidden, dq, dk, dv))

    terms = lax.all_to_all(zh_message(terms, nzh), "zh", 0, 0, tiled=True)
    terms = lax.all_to_all(spread(terms, nzl * CORES), ("zl", "core"), 0, 0, tiled=True)
    depth = nzh * CORES * slots
    weights = weight_terms(hidden, terms, depth).reshape(groups, SUB, width)
    weights = lax.all_to_all(weights, ("dp", "x"), 0, 0, tiled=True)
    beacon_dk, beacon_dv, weight_grad = finish(place, terms, weights, nzl, slots, depth, rows_out)
    return (dq[None], dk[None], dv[None], beacon_dk[None], beacon_dv[None], weight_grad)


def solution(mesh):
    ndp, nx, nzh, nzl = grid_of(mesh)
    fine = Mesh(
        mesh.devices.reshape(ndp, nx, nzh, nzl, CORES), ("dp", "x", "zh", "zl", "core")
    )
    seq = ("x", "zh", "zl", "core")
    split = P("dp", seq, None)
    return jax.shard_map(
        functools.partial(per_device, nx, nzh, nzl),
        mesh=fine,
        in_specs=(split,) * 7 + (P(), P()),
        out_specs=(split,) * 5 + (P(("dp",) + seq, None),),
        check_vma=False,
    )
```

```python
import functools
import math

import jax
import jax.numpy as jnp
from jax import lax
from jax.experimental import pallas as pl
from jax.experimental.pallas import tpu as pltpu
from jax.sharding import Mesh
from jax.sharding import PartitionSpec as P

QH = 14
KVH = 2
HD = 128
GROUPS = QH // KVH
NEG = -1e30
SCALE = 1.0 / math.sqrt(HD)
LOG2E = math.log2(math.e)
CORES = 2
SUB = 8
HEADS = 7
F32 = jnp.float32
BF16 = jnp.bfloat16


def grid_of(mesh):
    dp, seq = mesh.devices.shape
    nx, nzl = (4, 4) if seq == 128 else (2, 2)
    return dp, nx, seq // (nx * nzl * CORES), nzl


def visible_bias(order_row, ratio_row, mine, slots, span):
    nseq = order_row.shape[1]
    t = lax.broadcasted_iota(jnp.int32, (nseq, nseq), 0)
    picks = jnp.where(order_row == t, 1.0, 0.0).astype(F32)
    rates = jnp.broadcast_to(ratio_row.astype(F32), (slots, nseq))
    rate = jnp.dot(rates, picks, preferred_element_type=F32)
    cost = jnp.where(order_row < mine, rate, 4.0 * span)
    slot = lax.broadcasted_iota(jnp.int32, (slots, nseq), 0)
    return jnp.where((slot + 1).astype(F32) * cost <= float(span), 0.0, NEG)


def attention_kernel(
    nx, nzh, nzl, slots,
    bias, mine, other, beacons,
    terms, dscores, own_probs,
    kcat, vcat, qcat, ucat, probs,
):
    span = mine.shape[0]
    wide = GROUPS * HD
    sides = (mine, other)
    for r, side in enumerate(sides):
        kcat[r, 0:span, :] = side[:, 2 * wide : 2 * wide + HD]
        vcat[r, 0:span, :] = side[:, 2 * wide + HD :]
        kcat[r, span:, :] = beacons[:, 0:HD]
        vcat[r, span:, :] = beacons[:, HD:]
        for h in range(GROUPS):
            at = (r * GROUPS + h) * span
            qcat[at : at + span, :] = side[:, h * HD : (h + 1) * HD]
            ucat[at : at + span, :] = side[:, wide + h * HD : wide + (h + 1) * HD]

    key_row = lax.broadcasted_iota(jnp.int32, (span, span), 0)
    query_col = lax.broadcasted_iota(jnp.int32, (span, span), 1)
    causal = key_row <= query_col
    contract_last = (((1,), (1,)), ((), ()))
    contract_first = (((0,), (0,)), ((), ()))

    for r in range(CORES):
        for h0 in range(0, GROUPS, HEADS):
            heads = min(HEADS, GROUPS - h0)
            lo = (r * GROUPS + h0) * span
            rows = slice(lo, lo + heads * span)
            s = lax.dot_general(
                kcat[r], qcat[rows, :], contract_last, preferred_element_type=F32
            )
            dp = lax.dot_general(
                vcat[r], ucat[rows, :], contract_last, preferred_element_type=F32
            )
            s = s * (SCALE * LOG2E)
            own = jnp.where(jnp.concatenate([causal] * heads, axis=1), s[0:span, :], NEG)
            far = s[span:, :] + jnp.concatenate([bias[r]] * heads, axis=1)
            s = jnp.concatenate([own, far], axis=0)
            top = jnp.max(s, axis=0, keepdims=True)
            e = jnp.exp2(s - top)
            inv = 1.0 / jnp.sum(e, axis=0, keepdims=True)
            delta = jnp.sum(e * dp, axis=0, keepdims=True) * inv
            p = e * inv
            own_probs[:, rows] = p[0:span, :].astype(BF16)
            probs[:, rows] = p[span:, :].astype(BF16)
            dscores[:, rows] = (p * (dp - delta)).astype(BF16)

    products = ((0, dscores[span:, :], qcat, SCALE), (1, probs[...], ucat, 1.0))
    for kind, left, right, scale in products:
        full = jnp.dot(left, right[...], preferred_element_type=F32) * scale
        count = full.shape[0]
        full = full.reshape(nx, nzh, nzl, CORES * slots, HD)
        full = jnp.swapaxes(full, 1, 2).reshape(count, HD)
        terms[:, kind * HD : (kind + 1) * HD] = full.astype(BF16)


def own_kernel(dscores, probs, mine, other, beacons, own_out, other_out, kcat, qcat, ucat):
    span = mine.shape[0]
    wide = GROUPS * HD
    kcat[span:, :] = beacons[:, 0:HD]
    for r, (side, out) in enumerate(((mine, own_out), (other, other_out))):
        kcat[0:span, :] = side[:, 2 * wide : 2 * wide + HD]
        for h in range(GROUPS):
            qcat[h * span : (h + 1) * span, :] = side[:, h * HD : (h + 1) * HD]
            ucat[h * span : (h + 1) * span, :] = side[:, wide + h * HD : wide + (h + 1) * HD]
        rows = slice(r * wide, (r + 1) * wide)
        part = jnp.dot(dscores[0:span, rows], qcat[...], preferred_element_type=F32)
        out[:, wide : wide + HD] = (part * SCALE).astype(BF16)
        part = jnp.dot(probs[:, rows], ucat[...], preferred_element_type=F32)
        out[:, wide + HD :] = part.astype(BF16)
        part = lax.dot_general(
            kcat[...], dscores[:, rows], (((0,), (0,)), ((), ())), preferred_element_type=F32
        ) * SCALE
        for h in range(GROUPS):
            lanes = slice(h * HD, (h + 1) * HD)
            out[:, lanes] = part[:, h * span : (h + 1) * span].T.astype(BF16)


def own_grads(dscores, probs, mine, other, beacons):
    span = mine.shape[0]
    keys, columns = dscores.shape
    shape = bf16(span, GROUPS * HD + 2 * HD)
    return small_call(
        own_kernel, "own_grads", [shape, shape], dscores, probs, mine, other, beacons,
        flops=2 * keys * columns * HD,
        scratch=[
            pltpu.VMEM((keys, HD), BF16),
            pltpu.VMEM((GROUPS * span, HD), BF16),
            pltpu.VMEM((GROUPS * span, HD), BF16),
        ],
    )


def attention(bias, mine, other, beacons, nx, nzh, nzl, slots):
    span = mine.shape[0]
    total, lanes = beacons.shape
    keys = span + total
    wide = GROUPS * HD
    return small_call(
        functools.partial(attention_kernel, nx, nzh, nzl, slots), "attention",
        [bf16(total, lanes), bf16(keys, CORES * wide), bf16(span, CORES * wide)],
        bias, mine, other, beacons,
        flops=4 * 2 * QH * span * keys * HD,
        scratch=[
            pltpu.VMEM((CORES, keys, HD), BF16),
            pltpu.VMEM((CORES, keys, HD), BF16),
            pltpu.VMEM((CORES * wide, HD), BF16),
            pltpu.VMEM((CORES * wide, HD), BF16),
            pltpu.VMEM((total, CORES * wide), BF16),
        ],
    )


def add_blocks(ref):
    total = ref[0].astype(F32)
    for i in range(1, ref.shape[0]):
        total = total + ref[i].astype(F32)
    return total


VMEM = pl.BlockSpec(memory_space=pltpu.VMEM)
SMEM = pl.BlockSpec(memory_space=pltpu.SMEM)


def small_call(kernel, name, outs, *args, flops=0, scratch=()):
    size = sum(a.size * a.dtype.itemsize for a in args)
    size += sum(o.size * jnp.dtype(o.dtype).itemsize for o in outs)
    return pl.pallas_call(
        kernel,
        in_specs=[SMEM if a.dtype == jnp.int32 else VMEM for a in args],
        out_specs=[VMEM for _ in outs],
        out_shape=outs,
        scratch_shapes=list(scratch),
        compiler_params=pltpu.CompilerParams(vmem_limit_bytes=48 * 1024 * 1024),
        cost_estimate=pl.CostEstimate(flops=flops, bytes_accessed=size, transcendentals=0),
        name=name,
    )(*args)


def bf16(*shape):
    return jax.ShapeDtypeStruct(shape, BF16)


def message_kernel(groups, nz, rows_out, keys_in, values_in, hidden_in, out, keys, values, hidden, sems):
    copies = [
        pltpu.make_async_copy(source, held, sems.at[i])
        for i, (source, held) in enumerate(
            ((hidden_in, hidden), (keys_in, keys), (values_in, values))
        )
    ]
    for copy in copies:
        copy.start()
    for copy in copies:
        copy.wait()
    slots, width = keys.shape
    chunk = hidden.shape[1] // groups
    pieces = [hidden[:, i * chunk : (i + 1) * chunk].astype(F32) for i in range(groups)]
    if groups * slots < HD:
        pieces.append(jnp.zeros((HD - groups * slots, chunk), F32))
    stacked = jnp.concatenate(pieces, axis=0).astype(BF16)
    row = lax.broadcasted_iota(jnp.int32, (nz * CORES * SUB, chunk), 0)
    column = lax.broadcasted_iota(jnp.int32, (nz * CORES * SUB, chunk), 1)
    item = row % SUB
    picks = (column == (row // SUB) * rows_out + item) & (item < rows_out)
    turned = lax.dot_general(
        jnp.where(picks, 1.0, 0.0).astype(BF16),
        stacked,
        (((1,), (1,)), ((), ())),
        preferred_element_type=F32,
    )
    both = []
    for core in range(CORES):
        lanes = slice(core * HD, (core + 1) * HD)
        both.append(jnp.concatenate([keys[:, lanes], values[:, lanes]], axis=1).astype(F32))
    out[:, 0:width] = jnp.concatenate(both * nz, axis=0).astype(BF16)
    out[:, width:] = turned.astype(BF16)


def message(keys, values, hidden, groups, nz, rows_out):
    slots, width = keys.shape
    anywhere = pl.BlockSpec(memory_space=pl.ANY)
    return pl.pallas_call(
        functools.partial(message_kernel, groups, nz, rows_out),
        in_specs=[anywhere] * 3,
        out_specs=VMEM,
        out_shape=bf16(nz * CORES * slots, width + HD),
        scratch_shapes=[
            *[pltpu.VMEM(a.shape, BF16) for a in (keys, values, hidden)],
            pltpu.SemaphoreType.DMA((3,)),
        ],
        compiler_params=pltpu.CompilerParams(vmem_limit_bytes=56 * 1024 * 1024),
        cost_estimate=pl.CostEstimate(
            flops=0, bytes_accessed=512 * 1024, transcendentals=0
        ),
        name="message",
    )(keys, values, hidden)


def split_kernel(place, q, up, k, v, mine, send):
    wide = GROUPS * HD
    core = place[2]
    for out, head in ((mine, core), (send, 1 - core)):
        lanes = pl.ds(pl.multiple_of(head * wide, HD), wide)
        out[:, 0:wide] = q[:, lanes]
        out[:, wide : 2 * wide] = up[:, lanes]
        lanes = pl.ds(pl.multiple_of(head * HD, HD), HD)
        out[:, 2 * wide : 2 * wide + HD] = k[:, lanes]
        out[:, 2 * wide + HD :] = v[:, lanes]


def split_heads(place, q, up, k, v):
    shape = bf16(q.shape[0], 2 * GROUPS * HD + 2 * HD)
    return small_call(split_kernel, "split_heads", [shape, shape], place, q, up, k, v)


def join_kernel(place, mine, got, dq, dk, dv):
    wide = GROUPS * HD
    core = place[2]
    for part, head in ((mine, core), (got, 1 - core)):
        dq[:, pl.ds(pl.multiple_of(head * wide, HD), wide)] = part[:, 0:wide]
        lanes = pl.ds(pl.multiple_of(head * HD, HD), HD)
        dk[:, lanes] = part[:, wide : wide + HD]
        dv[:, lanes] = part[:, wide + HD :]


def join_heads(place, mine, got):
    span = mine.shape[0]
    shapes = [bf16(span, QH * HD), bf16(span, KVH * HD), bf16(span, KVH * HD)]
    return small_call(join_kernel, "join_heads", shapes, place, mine, got)


def mask_kernel(nz, slots, span, place, order_s, order_row, ratio_row, bias):
    core = place[2]
    first = (place[0] * nz + place[1]) * CORES
    for r, index in enumerate((first + core, first + 1 - core)):
        owners = visible_bias(order_row[...], ratio_row[...], order_s[index], slots, span)
        for j in range(owners.shape[1]):
            tile = jnp.broadcast_to(owners[:, j : j + 1], (slots, HD))
            bias[r, j * slots : (j + 1) * slots, :] = tile


def mask(place, order, ratio, nz, slots, span):
    nseq = order.shape[0]
    return pl.pallas_call(
        functools.partial(mask_kernel, nz, slots, span),
        in_specs=[SMEM, SMEM, VMEM, VMEM],
        out_specs=VMEM,
        out_shape=jax.ShapeDtypeStruct((CORES, nseq * slots, HD), F32),
        compiler_params=pltpu.CompilerParams(vmem_limit_bytes=32 * 1024 * 1024),
        cost_estimate=pl.CostEstimate(
            flops=0, bytes_accessed=2 * 1024 * 1024, transcendentals=0
        ),
        name="mask",
    )(place, order, order.reshape(1, nseq), ratio.reshape(1, nseq))


def turn_kernel(groups, nzh, nzl, slots, got, out):
    count = groups * SUB
    width = nzh * nzl * CORES * slots
    row = lax.broadcasted_iota(jnp.int32, (count, HD), 0)
    lane = lax.broadcasted_iota(jnp.int32, (count, HD), 1)
    same = lane // slots == row // SUB
    from_lane = lax.broadcasted_iota(jnp.int32, (HD, width), 0)
    to_lane = lax.broadcasted_iota(jnp.int32, (HD, width), 1)
    total = jnp.zeros((count, width), F32)
    for zh in range(nzh):
        for zl in range(nzl):
            for c in range(CORES):
                source = (zh * nzl + zl) * CORES + c
                target = (zl * nzh + zh) * CORES + c
                block = got[source * SUB : (source + 1) * SUB, :].astype(F32)
                block = jnp.where(same, jnp.concatenate([block] * groups, axis=0), 0.0)
                put = to_lane == target * slots + from_lane % slots
                total = total + jnp.dot(
                    block.astype(BF16),
                    jnp.where(put, 1.0, 0.0).astype(BF16),
                    preferred_element_type=F32,
                )
    out[...] = total.astype(BF16)


def turn(got, groups, nzh, nzl, slots):
    shape = bf16(groups * SUB, nzh * nzl * CORES * slots)
    kernel = functools.partial(turn_kernel, groups, nzh, nzl, slots)
    return small_call(kernel, "turn", [shape], got)[0]


def zh_kernel(got, out):
    total = add_blocks(got)
    rows = total.shape[0]
    each = rows // out.shape[0]
    keys = total[:, 0:HD].astype(BF16)
    for zh in range(out.shape[0]):
        out[zh, 0:rows, :] = keys
        out[zh, rows:, :] = total[zh * each : (zh + 1) * each, HD:].astype(BF16)


def zh_message(got, nzh):
    _, rows, _ = got.shape
    return small_call(zh_kernel, "zh_message", [bf16(nzh, rows + rows // nzh, HD)], got)[0]


def spread_kernel(got, out):
    total = add_blocks(got).astype(BF16)
    for i in range(out.shape[0]):
        out[i] = total


def spread(got, peers):
    return small_call(spread_kernel, "spread", [bf16(peers, *got.shape[1:])], got)[0]


def weight_kernel(rows, hidden, got, out):
    pairs = []
    for zl in range(got.shape[0] // CORES):
        heads = [got[zl * CORES + c, 0:rows, :] for c in range(CORES)]
        pairs.append(jnp.concatenate(heads, axis=1))
    keys = jnp.concatenate(pairs, axis=0)
    out[...] = jnp.dot(hidden[...], keys, preferred_element_type=F32).astype(BF16)


def weight_terms(hidden, got, rows):
    count, depth = hidden.shape
    return small_call(
        functools.partial(weight_kernel, rows), "weight_terms", [bf16(count, CORES * HD)],
        hidden, got, flops=2 * count * depth * CORES * HD,
    )[0]


def finish_kernel(slots, rows, got, weights, keys, values, weight_grad, held):
    zh, zl, core = (lax.axis_index(axis) for axis in ("zh", "zl", "core"))
    key_row = pl.multiple_of((zh * CORES + core) * slots, slots)
    value_row = pl.multiple_of(rows + core * slots, slots)
    for c in range(CORES):
        held[c] = got[pl.ds(zl * CORES + c, 1)][0].astype(F32)
        lanes = slice(c * HD, (c + 1) * HD)
        keys[:, lanes] = held[c, pl.ds(key_row, slots), :].astype(BF16)
        values[:, lanes] = held[c, pl.ds(value_row, slots), :].astype(BF16)
    weight_grad[...] = add_blocks(weights)[0 : weight_grad.shape[0], :]


def finish(got, weights, slots, rows, rows_out):
    width = weights.shape[2]
    return small_call(
        functools.partial(finish_kernel, slots, rows), "finish",
        [
            bf16(slots, width),
            bf16(slots, width),
            jax.ShapeDtypeStruct((rows_out, width), F32),
        ],
        got, weights, scratch=[pltpu.VMEM((CORES, *got.shape[1:]), F32)],
    )


def per_device(
    nx, nzh, nzl,
    queries, keys, values, grad_out, beacon_keys, beacon_values, beacon_hidden, order, ratio,
):
    ndp = lax.axis_size("dp")
    nz = nzh * nzl
    span = queries.shape[1]
    slots, width = beacon_keys.shape[1:]
    model = beacon_hidden.shape[2]
    groups = ndp * nx
    rows_out = model // (groups * nz * CORES)
    swap = [(0, 1), (1, 0)]
    z_index = lax.axis_index("zh") * nzl + lax.axis_index("zl")
    place = jnp.stack([lax.axis_index("x"), z_index, lax.axis_index("core")]).astype(jnp.int32)

    first = message(beacon_keys[0], beacon_values[0], beacon_hidden[0], groups, nz, rows_out)
    first = first.reshape(nz * CORES, slots, width + HD)
    first = lax.all_to_all(first, ("zh", "zl", "core"), 0, 0, tiled=True)
    mine, send = split_heads(place, queries[0], grad_out[0], keys[0], values[0])
    other = lax.ppermute(send, "core", swap)
    bias = mask(place, order, ratio, nz, slots, span)
    first, mine, other, bias = lax.optimization_barrier((first, mine, other, bias))

    beacons = first[:, :, :width].reshape(1, nz * CORES * slots, width)
    beacons = jnp.broadcast_to(beacons, (nx, nz * CORES * slots, width))
    beacons = lax.all_to_all(beacons, "x", 0, 0, tiled=True)
    beacons = beacons.reshape(nx * nz * CORES * slots, width)

    terms, dscores, probs = attention(bias, mine, other, beacons, nx, nzh, nzl, slots)

    terms = terms.reshape(nx * nzl, nzh * CORES * slots, width)
    terms = lax.all_to_all(terms, ("x", "zl"), 0, 0, tiled=True)
    own_out, other_out = own_grads(dscores, probs, mine, other, beacons)
    dq, dk, dv = join_heads(place, own_out, lax.ppermute(other_out, "core", swap))
    hidden = first[:, :, width:].reshape(nz * CORES * slots, HD)
    hidden = turn(hidden, groups, nzh, nzl, slots)
    terms, hidden, dq, dk, dv = lax.optimization_barrier((terms, hidden, dq, dk, dv))

    terms = lax.all_to_all(zh_message(terms, nzh), "zh", 0, 0, tiled=True)
    terms = lax.all_to_all(spread(terms, nzl * CORES), ("zl", "core"), 0, 0, tiled=True)
    depth = nzh * CORES * slots
    weights = weight_terms(hidden, terms, depth).reshape(groups, SUB, width)
    weights = lax.all_to_all(weights, ("dp", "x"), 0, 0, tiled=True)
    beacon_dk, beacon_dv, weight_grad = finish(terms, weights, slots, depth, rows_out)
    return (dq[None], dk[None], dv[None], beacon_dk[None], beacon_dv[None], weight_grad)


def solution(mesh):
    ndp, nx, nzh, nzl = grid_of(mesh)
    fine = Mesh(
        mesh.devices.reshape(ndp, nx, nzh, nzl, CORES), ("dp", "x", "zh", "zl", "core")
    )
    seq = ("x", "zh", "zl", "core")
    split = P("dp", seq, None)
    return jax.shard_map(
        functools.partial(per_device, nx, nzh, nzl),
        mesh=fine,
        in_specs=(split,) * 7 + (P(), P()),
        out_specs=(split,) * 5 + (P(("dp",) + seq, None),),
        check_vma=False,
    )
```

```python
import functools
import math

import jax
import jax.numpy as jnp
from jax import lax
from jax.experimental import pallas as pl
from jax.experimental.pallas import tpu as pltpu
from jax.sharding import Mesh
from jax.sharding import PartitionSpec as P

QH = 14
KVH = 2
HD = 128
GROUPS = QH // KVH
NEG = -1e30
SCALE = 1.0 / math.sqrt(HD)
LOG2E = math.log2(math.e)
CORES = 2
SUB = 8
HEADS = 7
F32 = jnp.float32
BF16 = jnp.bfloat16


def grid_of(mesh):
    dp, seq = mesh.devices.shape
    nx, nzl = (4, 4) if seq == 128 else (2, 2)
    return dp, nx, seq // (nx * nzl * CORES), nzl


def visible_bias(order_row, ratio_row, mine, slots, span):
    nseq = order_row.shape[1]
    t = lax.broadcasted_iota(jnp.int32, (nseq, nseq), 0)
    picks = jnp.where(order_row == t, 1.0, 0.0).astype(F32)
    rates = jnp.broadcast_to(ratio_row.astype(F32), (slots, nseq))
    rate = jnp.dot(rates, picks, preferred_element_type=F32)
    cost = jnp.where(order_row < mine, rate, 4.0 * span)
    slot = lax.broadcasted_iota(jnp.int32, (slots, nseq), 0)
    return jnp.where((slot + 1).astype(F32) * cost <= float(span), 0.0, NEG)


def attention_kernel(
    nx, nzh, nzl, slots,
    bias, mine, other, beacons,
    terms, dscores, own_probs,
    kcat, vcat, qcat, ucat, probs,
):
    span = mine.shape[0]
    wide = GROUPS * HD
    sides = (mine, other)
    for r, side in enumerate(sides):
        kcat[r, 0:span, :] = side[:, 2 * wide : 2 * wide + HD]
        vcat[r, 0:span, :] = side[:, 2 * wide + HD :]
        kcat[r, span:, :] = beacons[:, 0:HD]
        vcat[r, span:, :] = beacons[:, HD:]
        for h in range(GROUPS):
            at = (r * GROUPS + h) * span
            qcat[at : at + span, :] = side[:, h * HD : (h + 1) * HD]
            ucat[at : at + span, :] = side[:, wide + h * HD : wide + (h + 1) * HD]

    key_row = lax.broadcasted_iota(jnp.int32, (span, span), 0)
    query_col = lax.broadcasted_iota(jnp.int32, (span, span), 1)
    causal = key_row <= query_col
    contract_last = (((1,), (1,)), ((), ()))
    contract_first = (((0,), (0,)), ((), ()))

    for r in range(CORES):
        for h0 in range(0, GROUPS, HEADS):
            heads = min(HEADS, GROUPS - h0)
            lo = (r * GROUPS + h0) * span
            rows = slice(lo, lo + heads * span)
            s = lax.dot_general(
                kcat[r], qcat[rows, :], contract_last, preferred_element_type=F32
            )
            dp = lax.dot_general(
                vcat[r], ucat[rows, :], contract_last, preferred_element_type=F32
            )
            s = s * (SCALE * LOG2E)
            own = jnp.where(jnp.concatenate([causal] * heads, axis=1), s[0:span, :], NEG)
            far = s[span:, :] + jnp.concatenate([bias[r]] * heads, axis=1)
            s = jnp.concatenate([own, far], axis=0)
            top = jnp.max(s, axis=0, keepdims=True)
            e = jnp.exp2(s - top)
            inv = 1.0 / jnp.sum(e, axis=0, keepdims=True)
            delta = jnp.sum(e * dp, axis=0, keepdims=True) * inv
            p = e * inv
            own_probs[:, rows] = p[0:span, :].astype(BF16)
            probs[:, rows] = p[span:, :].astype(BF16)
            dscores[:, rows] = (p * (dp - delta)).astype(BF16)

    products = ((0, dscores[span:, :], qcat, SCALE), (1, probs[...], ucat, 1.0))
    for kind, left, right, scale in products:
        full = jnp.dot(left, right[...], preferred_element_type=F32) * scale
        count = full.shape[0]
        full = full.reshape(nx, nzh, nzl, CORES * slots, HD)
        full = jnp.swapaxes(full, 1, 2).reshape(count, HD)
        terms[:, kind * HD : (kind + 1) * HD] = full.astype(BF16)


def own_kernel(dscores, probs, mine, other, beacons, own_out, other_out, kcat, qcat, ucat):
    span = mine.shape[0]
    wide = GROUPS * HD

    def rows_of(side, out):
        kcat[0:span, :] = side[:, 2 * wide : 2 * wide + HD]
        kcat[span:, :] = beacons[...]
        for h in range(GROUPS):
            qcat[h * span : (h + 1) * span, :] = side[:, h * HD : (h + 1) * HD]
            ucat[h * span : (h + 1) * span, :] = side[:, wide + h * HD : wide + (h + 1) * HD]
        part = jnp.dot(dscores[0:span, :], qcat[...], preferred_element_type=F32)
        out[:, wide : wide + HD] = (part * SCALE).astype(BF16)
        part = jnp.dot(probs[...], ucat[...], preferred_element_type=F32)
        out[:, wide + HD :] = part.astype(BF16)
        part = lax.dot_general(
            kcat[...], dscores[...], (((0,), (0,)), ((), ())), preferred_element_type=F32
        ) * SCALE
        for h in range(GROUPS):
            lanes = slice(h * HD, (h + 1) * HD)
            out[:, lanes] = part[:, h * span : (h + 1) * span].T.astype(BF16)

    pl.when(pl.program_id(0) == 0)(lambda: rows_of(mine, own_out))
    pl.when(pl.program_id(0) == 1)(lambda: rows_of(other, other_out))


def own_grads(dscores, probs, mine, other, beacons):
    span = mine.shape[0]
    keys, columns = dscores.shape
    wide = GROUPS * HD
    shape = bf16(span, wide + 2 * HD)
    whole = pl.BlockSpec(mine.shape, lambda r: (0, 0))
    result = pl.BlockSpec(shape.shape, lambda r: (0, 0))
    return pl.pallas_call(
        own_kernel,
        grid=(CORES,),
        in_specs=[
            pl.BlockSpec((keys, wide), lambda r: (0, r)),
            pl.BlockSpec((span, wide), lambda r: (0, r)),
            whole,
            whole,
            pl.BlockSpec((beacons.shape[0], HD), lambda r: (0, 0)),
        ],
        out_specs=[result, result],
        out_shape=[shape, shape],
        scratch_shapes=[
            pltpu.VMEM((keys, HD), BF16),
            pltpu.VMEM((wide, HD), BF16),
            pltpu.VMEM((wide, HD), BF16),
        ],
        compiler_params=pltpu.CompilerParams(vmem_limit_bytes=48 * 1024 * 1024),
        cost_estimate=pl.CostEstimate(
            flops=2 * keys * columns * HD, bytes_accessed=6 * 1024 * 1024, transcendentals=0
        ),
        name="own_grads",
    )(dscores, probs, mine, other, beacons)


def attention(bias, mine, other, beacons, nx, nzh, nzl, slots):
    span = mine.shape[0]
    total, lanes = beacons.shape
    keys = span + total
    wide = GROUPS * HD
    return small_call(
        functools.partial(attention_kernel, nx, nzh, nzl, slots), "attention",
        [bf16(total, lanes), bf16(keys, CORES * wide), bf16(span, CORES * wide)],
        bias, mine, other, beacons,
        flops=4 * 2 * QH * span * keys * HD,
        scratch=[
            pltpu.VMEM((CORES, keys, HD), BF16),
            pltpu.VMEM((CORES, keys, HD), BF16),
            pltpu.VMEM((CORES * wide, HD), BF16),
            pltpu.VMEM((CORES * wide, HD), BF16),
            pltpu.VMEM((total, CORES * wide), BF16),
        ],
    )


def add_blocks(ref):
    total = ref[0].astype(F32)
    for i in range(1, ref.shape[0]):
        total = total + ref[i].astype(F32)
    return total


VMEM = pl.BlockSpec(memory_space=pltpu.VMEM)
SMEM = pl.BlockSpec(memory_space=pltpu.SMEM)


def small_call(kernel, name, outs, *args, flops=0, scratch=()):
    size = sum(a.size * a.dtype.itemsize for a in args)
    size += sum(o.size * jnp.dtype(o.dtype).itemsize for o in outs)
    return pl.pallas_call(
        kernel,
        in_specs=[SMEM if a.dtype == jnp.int32 else VMEM for a in args],
        out_specs=[VMEM for _ in outs],
        out_shape=outs,
        scratch_shapes=list(scratch),
        compiler_params=pltpu.CompilerParams(vmem_limit_bytes=48 * 1024 * 1024),
        cost_estimate=pl.CostEstimate(flops=flops, bytes_accessed=size, transcendentals=0),
        name=name,
    )(*args)


def bf16(*shape):
    return jax.ShapeDtypeStruct(shape, BF16)


def message_kernel(groups, nz, rows_out, keys_in, values_in, hidden_in, out, keys, values, hidden, sems):
    copies = [
        pltpu.make_async_copy(source, held, sems.at[i])
        for i, (source, held) in enumerate(
            ((hidden_in, hidden), (keys_in, keys), (values_in, values))
        )
    ]
    for copy in copies:
        copy.start()
    for copy in copies:
        copy.wait()
    slots, width = keys.shape
    chunk = hidden.shape[1] // groups
    pieces = [hidden[:, i * chunk : (i + 1) * chunk].astype(F32) for i in range(groups)]
    if groups * slots < HD:
        pieces.append(jnp.zeros((HD - groups * slots, chunk), F32))
    stacked = jnp.concatenate(pieces, axis=0).astype(BF16)
    row = lax.broadcasted_iota(jnp.int32, (nz * CORES * SUB, chunk), 0)
    column = lax.broadcasted_iota(jnp.int32, (nz * CORES * SUB, chunk), 1)
    item = row % SUB
    picks = (column == (row // SUB) * rows_out + item) & (item < rows_out)
    turned = lax.dot_general(
        jnp.where(picks, 1.0, 0.0).astype(BF16),
        stacked,
        (((1,), (1,)), ((), ())),
        preferred_element_type=F32,
    )
    both = []
    for core in range(CORES):
        lanes = slice(core * HD, (core + 1) * HD)
        both.append(jnp.concatenate([keys[:, lanes], values[:, lanes]], axis=1).astype(F32))
    out[:, 0:width] = jnp.concatenate(both * nz, axis=0).astype(BF16)
    out[:, width:] = turned.astype(BF16)


def message(keys, values, hidden, groups, nz, rows_out):
    slots, width = keys.shape
    anywhere = pl.BlockSpec(memory_space=pl.ANY)
    return pl.pallas_call(
        functools.partial(message_kernel, groups, nz, rows_out),
        in_specs=[anywhere] * 3,
        out_specs=VMEM,
        out_shape=bf16(nz * CORES * slots, width + HD),
        scratch_shapes=[
            *[pltpu.VMEM(a.shape, BF16) for a in (keys, values, hidden)],
            pltpu.SemaphoreType.DMA((3,)),
        ],
        compiler_params=pltpu.CompilerParams(vmem_limit_bytes=56 * 1024 * 1024),
        cost_estimate=pl.CostEstimate(
            flops=0, bytes_accessed=512 * 1024, transcendentals=0
        ),
        name="message",
    )(keys, values, hidden)


def split_kernel(q, up, k, v, mine, send):
    wide = GROUPS * HD
    core = lax.axis_index("core")
    for out, head in ((mine, core), (send, 1 - core)):
        lanes = pl.ds(pl.multiple_of(head * wide, HD), wide)
        out[:, 0:wide] = q[:, lanes]
        out[:, wide : 2 * wide] = up[:, lanes]
        lanes = pl.ds(pl.multiple_of(head * HD, HD), HD)
        out[:, 2 * wide : 2 * wide + HD] = k[:, lanes]
        out[:, 2 * wide + HD :] = v[:, lanes]


def split_heads(q, up, k, v):
    shape = bf16(q.shape[0], 2 * GROUPS * HD + 2 * HD)
    return small_call(split_kernel, "split_heads", [shape, shape], q, up, k, v)


def join_kernel(mine, got, dq, dk, dv):
    wide = GROUPS * HD
    core = lax.axis_index("core")
    for part, head in ((mine, core), (got, 1 - core)):
        dq[:, pl.ds(pl.multiple_of(head * wide, HD), wide)] = part[:, 0:wide]
        lanes = pl.ds(pl.multiple_of(head * HD, HD), HD)
        dk[:, lanes] = part[:, wide : wide + HD]
        dv[:, lanes] = part[:, wide + HD :]


def join_heads(mine, got):
    span = mine.shape[0]
    shapes = [bf16(span, QH * HD), bf16(span, KVH * HD), bf16(span, KVH * HD)]
    return small_call(join_kernel, "join_heads", shapes, mine, got)


def mask_kernel(nz, nzl, slots, span, order_s, order_row, ratio_row, bias):
    x, zh, zl, core = (lax.axis_index(axis) for axis in ("x", "zh", "zl", "core"))
    first = (x * nz + zh * nzl + zl) * CORES
    for r, index in enumerate((first + core, first + 1 - core)):
        owners = visible_bias(order_row[...], ratio_row[...], order_s[index], slots, span)
        for j in range(owners.shape[1]):
            tile = jnp.broadcast_to(owners[:, j : j + 1], (slots, HD))
            bias[r, j * slots : (j + 1) * slots, :] = tile


def mask(order, ratio, nz, nzl, slots, span):
    nseq = order.shape[0]
    return pl.pallas_call(
        functools.partial(mask_kernel, nz, nzl, slots, span),
        in_specs=[SMEM, VMEM, VMEM],
        out_specs=VMEM,
        out_shape=jax.ShapeDtypeStruct((CORES, nseq * slots, HD), F32),
        compiler_params=pltpu.CompilerParams(vmem_limit_bytes=32 * 1024 * 1024),
        cost_estimate=pl.CostEstimate(
            flops=0, bytes_accessed=2 * 1024 * 1024, transcendentals=0
        ),
        name="mask",
    )(order, order.reshape(1, nseq), ratio.reshape(1, nseq))


def turn_kernel(groups, nzh, nzl, slots, got, out):
    count = groups * SUB
    width = nzh * nzl * CORES * slots
    row = lax.broadcasted_iota(jnp.int32, (count, HD), 0)
    lane = lax.broadcasted_iota(jnp.int32, (count, HD), 1)
    same = lane // slots == row // SUB
    from_lane = lax.broadcasted_iota(jnp.int32, (HD, width), 0)
    to_lane = lax.broadcasted_iota(jnp.int32, (HD, width), 1)
    total = jnp.zeros((count, width), F32)
    for zh in range(nzh):
        for zl in range(nzl):
            for c in range(CORES):
                source = (zh * nzl + zl) * CORES + c
                target = (zl * nzh + zh) * CORES + c
                block = got[source * SUB : (source + 1) * SUB, :].astype(F32)
                block = jnp.where(same, jnp.concatenate([block] * groups, axis=0), 0.0)
                put = to_lane == target * slots + from_lane % slots
                total = total + jnp.dot(
                    block.astype(BF16),
                    jnp.where(put, 1.0, 0.0).astype(BF16),
                    preferred_element_type=F32,
                )
    out[...] = total.astype(BF16)


def turn(got, groups, nzh, nzl, slots):
    shape = bf16(groups * SUB, nzh * nzl * CORES * slots)
    kernel = functools.partial(turn_kernel, groups, nzh, nzl, slots)
    return small_call(kernel, "turn", [shape], got)[0]


def zh_kernel(got, out):
    total = add_blocks(got)
    rows = total.shape[0]
    each = rows // out.shape[0]
    keys = total[:, 0:HD].astype(BF16)
    for zh in range(out.shape[0]):
        out[zh, 0:rows, :] = keys
        out[zh, rows:, :] = total[zh * each : (zh + 1) * each, HD:].astype(BF16)


def zh_message(got, nzh):
    _, rows, _ = got.shape
    return small_call(zh_kernel, "zh_message", [bf16(nzh, rows + rows // nzh, HD)], got)[0]


def spread_kernel(got, out):
    total = add_blocks(got).astype(BF16)
    for i in range(out.shape[0]):
        out[i] = total


def spread(got, peers):
    return small_call(spread_kernel, "spread", [bf16(peers, *got.shape[1:])], got)[0]


def weight_kernel(rows, hidden, got, out):
    pairs = []
    for zl in range(got.shape[0] // CORES):
        heads = [got[zl * CORES + c, 0:rows, :] for c in range(CORES)]
        pairs.append(jnp.concatenate(heads, axis=1))
    keys = jnp.concatenate(pairs, axis=0)
    out[...] = jnp.dot(hidden[...], keys, preferred_element_type=F32).astype(BF16)


def weight_terms(hidden, got, rows):
    count, depth = hidden.shape
    return small_call(
        functools.partial(weight_kernel, rows), "weight_terms", [bf16(count, CORES * HD)],
        hidden, got, flops=2 * count * depth * CORES * HD,
    )[0]


def finish_kernel(slots, rows, got, weights, keys, values, weight_grad, held):
    zh, zl, core = (lax.axis_index(axis) for axis in ("zh", "zl", "core"))
    key_row = pl.multiple_of((zh * CORES + core) * slots, slots)
    value_row = pl.multiple_of(rows + core * slots, slots)
    for c in range(CORES):
        held[c] = got[pl.ds(zl * CORES + c, 1)][0].astype(F32)
        lanes = slice(c * HD, (c + 1) * HD)
        keys[:, lanes] = held[c, pl.ds(key_row, slots), :].astype(BF16)
        values[:, lanes] = held[c, pl.ds(value_row, slots), :].astype(BF16)
    weight_grad[...] = add_blocks(weights)[0 : weight_grad.shape[0], :]


def finish(got, weights, slots, rows, rows_out):
    width = weights.shape[2]
    return small_call(
        functools.partial(finish_kernel, slots, rows), "finish",
        [
            bf16(slots, width),
            bf16(slots, width),
            jax.ShapeDtypeStruct((rows_out, width), F32),
        ],
        got, weights, scratch=[pltpu.VMEM((CORES, *got.shape[1:]), F32)],
    )


def near_groups(nx, nzh, nzl):
    groups = []
    for core in range(CORES):
        for zh in range(nzh):
            members = []
            for x in range(nx):
                for zl in range(nzl):
                    place = zh if core == 0 or zl >= nzl // 2 else (zh + 1) % nzh
                    members.append(((x * nzh + place) * nzl + zl) * CORES + core)
            groups.append(members)
    return groups


def per_device(
    nx, nzh, nzl,
    queries, keys, values, grad_out, beacon_keys, beacon_values, beacon_hidden, order, ratio,
):
    ndp = lax.axis_size("dp")
    nz = nzh * nzl
    span = queries.shape[1]
    slots, width = beacon_keys.shape[1:]
    model = beacon_hidden.shape[2]
    groups = ndp * nx
    rows_out = model // (groups * nz * CORES)
    swap = [(0, 1), (1, 0)]

    first = message(beacon_keys[0], beacon_values[0], beacon_hidden[0], groups, nz, rows_out)
    first = first.reshape(nz * CORES, slots, width + HD)
    first = lax.all_to_all(first, ("zh", "zl", "core"), 0, 0, tiled=True)
    mine, send = split_heads(queries[0], grad_out[0], keys[0], values[0])
    other = lax.ppermute(send, "core", swap)
    bias = mask(order, ratio, nz, nzl, slots, span)
    first, mine, other, bias = lax.optimization_barrier((first, mine, other, bias))

    beacons = first[:, :, :width].reshape(1, nz * CORES * slots, width)
    beacons = jnp.broadcast_to(beacons, (nx, nz * CORES * slots, width))
    beacons = lax.all_to_all(beacons, "x", 0, 0, tiled=True)
    beacons = beacons.reshape(nx * nz * CORES * slots, width)

    terms, dscores, probs = attention(bias, mine, other, beacons, nx, nzh, nzl, slots)

    terms = terms.reshape(nx * nzl, nzh * CORES * slots, width)
    terms = lax.all_to_all(
        terms, ("x", "zh", "zl", "core"), 0, 0, tiled=True,
        axis_index_groups=near_groups(nx, nzh, nzl),
    )
    own_out, other_out = own_grads(dscores, probs, mine, other, beacons)
    dq, dk, dv = join_heads(own_out, lax.ppermute(other_out, "core", swap))
    hidden = first[:, :, width:].reshape(nz * CORES * slots, HD)
    hidden = turn(hidden, groups, nzh, nzl, slots)
    terms, hidden, dq, dk, dv = lax.optimization_barrier((terms, hidden, dq, dk, dv))

    terms = lax.all_to_all(zh_message(terms, nzh), "zh", 0, 0, tiled=True)
    terms = lax.all_to_all(spread(terms, nzl * CORES), ("zl", "core"), 0, 0, tiled=True)
    depth = nzh * CORES * slots
    weights = weight_terms(hidden, terms, depth).reshape(groups, SUB, width)
    weights = lax.all_to_all(weights, ("dp", "x"), 0, 0, tiled=True)
    beacon_dk, beacon_dv, weight_grad = finish(terms, weights, slots, depth, rows_out)
    return (dq[None], dk[None], dv[None], beacon_dk[None], beacon_dv[None], weight_grad)


def solution(mesh):
    ndp, nx, nzh, nzl = grid_of(mesh)
    fine = Mesh(
        mesh.devices.reshape(ndp, nx, nzh, nzl, CORES), ("dp", "x", "zh", "zl", "core")
    )
    seq = ("x", "zh", "zl", "core")
    split = P("dp", seq, None)
    return jax.shard_map(
        functools.partial(per_device, nx, nzh, nzl),
        mesh=fine,
        in_specs=(split,) * 7 + (P(), P()),
        out_specs=(split,) * 5 + (P(("dp",) + seq, None),),
        check_vma=False,
    )
```

```python
import functools
import math

import jax
import jax.numpy as jnp
from jax import lax
from jax.experimental import pallas as pl
from jax.experimental.pallas import tpu as pltpu
from jax.sharding import Mesh
from jax.sharding import PartitionSpec as P

QH = 14
KVH = 2
HD = 128
GROUPS = QH // KVH
NEG = -1e30
SCALE = 1.0 / math.sqrt(HD)
LOG2E = math.log2(math.e)
CORES = 2
SUB = 8
HEADS = 7
F32 = jnp.float32
BF16 = jnp.bfloat16


def grid_of(mesh):
    dp, seq = mesh.devices.shape
    nx, nzl = (4, 4) if seq == 128 else (2, 2)
    return dp, nx, seq // (nx * nzl * CORES), nzl


def visible_bias(order_row, ratio_row, mine, slots, span):
    nseq = order_row.shape[1]
    t = lax.broadcasted_iota(jnp.int32, (nseq, nseq), 0)
    picks = jnp.where(order_row == t, 1.0, 0.0).astype(F32)
    rates = jnp.broadcast_to(ratio_row.astype(F32), (slots, nseq))
    rate = jnp.dot(rates, picks, preferred_element_type=F32)
    cost = jnp.where(order_row < mine, rate, 4.0 * span)
    slot = lax.broadcasted_iota(jnp.int32, (slots, nseq), 0)
    return jnp.where((slot + 1).astype(F32) * cost <= float(span), 0.0, NEG)


def attention_kernel(
    nx, nzh, nzl, slots,
    bias, mine, other, beacons,
    terms, dscores, own_probs,
    kcat, vcat, qcat, ucat, probs,
):
    span = mine.shape[0]
    wide = GROUPS * HD
    sides = (mine, other)
    for r, side in enumerate(sides):
        kcat[r, 0:span, :] = side[:, 2 * wide : 2 * wide + HD]
        vcat[r, 0:span, :] = side[:, 2 * wide + HD :]
        kcat[r, span:, :] = beacons[:, 0:HD]
        vcat[r, span:, :] = beacons[:, HD:]
        for h in range(GROUPS):
            at = (r * GROUPS + h) * span
            qcat[at : at + span, :] = side[:, h * HD : (h + 1) * HD]
            ucat[at : at + span, :] = side[:, wide + h * HD : wide + (h + 1) * HD]

    key_row = lax.broadcasted_iota(jnp.int32, (span, span), 0)
    query_col = lax.broadcasted_iota(jnp.int32, (span, span), 1)
    causal = key_row <= query_col
    contract_last = (((1,), (1,)), ((), ()))
    contract_first = (((0,), (0,)), ((), ()))

    for r in range(CORES):
        for h0 in range(0, GROUPS, HEADS):
            heads = min(HEADS, GROUPS - h0)
            lo = (r * GROUPS + h0) * span
            rows = slice(lo, lo + heads * span)
            s = lax.dot_general(
                kcat[r], qcat[rows, :], contract_last, preferred_element_type=F32
            )
            dp = lax.dot_general(
                vcat[r], ucat[rows, :], contract_last, preferred_element_type=F32
            )
            s = s * (SCALE * LOG2E)
            own = jnp.where(jnp.concatenate([causal] * heads, axis=1), s[0:span, :], NEG)
            far = s[span:, :] + jnp.concatenate([bias[r]] * heads, axis=1)
            s = jnp.concatenate([own, far], axis=0)
            top = jnp.max(s, axis=0, keepdims=True)
            e = jnp.exp2(s - top)
            inv = 1.0 / jnp.sum(e, axis=0, keepdims=True)
            delta = jnp.sum(e * dp, axis=0, keepdims=True) * inv
            p = e * inv
            own_probs[:, rows] = p[0:span, :].astype(BF16)
            probs[:, rows] = p[span:, :].astype(BF16)
            dscores[:, rows] = (p * (dp - delta)).astype(BF16)

    products = ((0, dscores[span:, :], qcat, SCALE), (1, probs[...], ucat, 1.0))
    for kind, left, right, scale in products:
        full = jnp.dot(left, right[...], preferred_element_type=F32) * scale
        count = full.shape[0]
        full = full.reshape(nx, nzh, nzl, CORES * slots, HD)
        full = jnp.swapaxes(full, 1, 2).reshape(count, HD)
        terms[:, kind * HD : (kind + 1) * HD] = full.astype(BF16)


def own_kernel(dscores, probs, mine, other, beacons, own_out, other_out, kcat, qcat, ucat):
    span = mine.shape[0]
    wide = GROUPS * HD

    def rows_of(side, out):
        kcat[0:span, :] = side[:, 2 * wide : 2 * wide + HD]
        kcat[span:, :] = beacons[...]
        for h in range(GROUPS):
            qcat[h * span : (h + 1) * span, :] = side[:, h * HD : (h + 1) * HD]
            ucat[h * span : (h + 1) * span, :] = side[:, wide + h * HD : wide + (h + 1) * HD]
        part = jnp.dot(dscores[0:span, :], qcat[...], preferred_element_type=F32)
        out[:, wide : wide + HD] = (part * SCALE).astype(BF16)
        part = jnp.dot(probs[...], ucat[...], preferred_element_type=F32)
        out[:, wide + HD :] = part.astype(BF16)
        part = lax.dot_general(
            kcat[...], dscores[...], (((0,), (0,)), ((), ())), preferred_element_type=F32
        ) * SCALE
        for h in range(GROUPS):
            lanes = slice(h * HD, (h + 1) * HD)
            out[:, lanes] = part[:, h * span : (h + 1) * span].T.astype(BF16)

    pl.when(pl.program_id(0) == 0)(lambda: rows_of(mine, own_out))
    pl.when(pl.program_id(0) == 1)(lambda: rows_of(other, other_out))


def own_grads(dscores, probs, mine, other, beacons):
    span = mine.shape[0]
    keys, columns = dscores.shape
    wide = GROUPS * HD
    shape = bf16(span, wide + 2 * HD)
    whole = pl.BlockSpec(mine.shape, lambda r: (0, 0))
    result = pl.BlockSpec(shape.shape, lambda r: (0, 0))
    return pl.pallas_call(
        own_kernel,
        grid=(CORES,),
        in_specs=[
            pl.BlockSpec((keys, wide), lambda r: (0, r)),
            pl.BlockSpec((span, wide), lambda r: (0, r)),
            whole,
            whole,
            pl.BlockSpec((beacons.shape[0], HD), lambda r: (0, 0)),
        ],
        out_specs=[result, result],
        out_shape=[shape, shape],
        scratch_shapes=[
            pltpu.VMEM((keys, HD), BF16),
            pltpu.VMEM((wide, HD), BF16),
            pltpu.VMEM((wide, HD), BF16),
        ],
        compiler_params=pltpu.CompilerParams(vmem_limit_bytes=48 * 1024 * 1024),
        cost_estimate=pl.CostEstimate(
            flops=2 * keys * columns * HD, bytes_accessed=6 * 1024 * 1024, transcendentals=0
        ),
        name="own_grads",
    )(dscores, probs, mine, other, beacons)


def attention(bias, mine, other, beacons, nx, nzh, nzl, slots):
    span = mine.shape[0]
    total, lanes = beacons.shape
    keys = span + total
    wide = GROUPS * HD
    return small_call(
        functools.partial(attention_kernel, nx, nzh, nzl, slots), "attention",
        [bf16(total, lanes), bf16(keys, CORES * wide), bf16(span, CORES * wide)],
        bias, mine, other, beacons,
        flops=4 * 2 * QH * span * keys * HD,
        scratch=[
            pltpu.VMEM((CORES, keys, HD), BF16),
            pltpu.VMEM((CORES, keys, HD), BF16),
            pltpu.VMEM((CORES * wide, HD), BF16),
            pltpu.VMEM((CORES * wide, HD), BF16),
            pltpu.VMEM((total, CORES * wide), BF16),
        ],
    )


def add_blocks(ref):
    total = ref[0].astype(F32)
    for i in range(1, ref.shape[0]):
        total = total + ref[i].astype(F32)
    return total


VMEM = pl.BlockSpec(memory_space=pltpu.VMEM)
SMEM = pl.BlockSpec(memory_space=pltpu.SMEM)


def small_call(kernel, name, outs, *args, flops=0, scratch=()):
    size = sum(a.size * a.dtype.itemsize for a in args)
    size += sum(o.size * jnp.dtype(o.dtype).itemsize for o in outs)
    return pl.pallas_call(
        kernel,
        in_specs=[SMEM if a.dtype == jnp.int32 else VMEM for a in args],
        out_specs=[VMEM for _ in outs],
        out_shape=outs,
        scratch_shapes=list(scratch),
        compiler_params=pltpu.CompilerParams(vmem_limit_bytes=48 * 1024 * 1024),
        cost_estimate=pl.CostEstimate(flops=flops, bytes_accessed=size, transcendentals=0),
        name=name,
    )(*args)


def bf16(*shape):
    return jax.ShapeDtypeStruct(shape, BF16)


def message_kernel(groups, nz, rows_out, keys_in, values_in, hidden_in, out, keys, values, hidden, sems):
    copies = [
        pltpu.make_async_copy(source, held, sems.at[i])
        for i, (source, held) in enumerate(
            ((hidden_in, hidden), (keys_in, keys), (values_in, values))
        )
    ]
    for copy in copies:
        copy.start()
    for copy in copies:
        copy.wait()
    slots, width = keys.shape
    chunk = hidden.shape[1] // groups
    pieces = [hidden[:, i * chunk : (i + 1) * chunk].astype(F32) for i in range(groups)]
    if groups * slots < HD:
        pieces.append(jnp.zeros((HD - groups * slots, chunk), F32))
    stacked = jnp.concatenate(pieces, axis=0).astype(BF16)
    row = lax.broadcasted_iota(jnp.int32, (nz * CORES * SUB, chunk), 0)
    column = lax.broadcasted_iota(jnp.int32, (nz * CORES * SUB, chunk), 1)
    item = row % SUB
    picks = (column == (row // SUB) * rows_out + item) & (item < rows_out)
    turned = lax.dot_general(
        jnp.where(picks, 1.0, 0.0).astype(BF16),
        stacked,
        (((1,), (1,)), ((), ())),
        preferred_element_type=F32,
    )
    both = []
    for core in range(CORES):
        lanes = slice(core * HD, (core + 1) * HD)
        both.append(jnp.concatenate([keys[:, lanes], values[:, lanes]], axis=1).astype(F32))
    out[:, 0:width] = jnp.concatenate(both * nz, axis=0).astype(BF16)
    out[:, width:] = turned.astype(BF16)


def message(keys, values, hidden, groups, nz, rows_out):
    slots, width = keys.shape
    anywhere = pl.BlockSpec(memory_space=pl.ANY)
    return pl.pallas_call(
        functools.partial(message_kernel, groups, nz, rows_out),
        in_specs=[anywhere] * 3,
        out_specs=VMEM,
        out_shape=bf16(nz * CORES * slots, width + HD),
        scratch_shapes=[
            *[pltpu.VMEM(a.shape, BF16) for a in (keys, values, hidden)],
            pltpu.SemaphoreType.DMA((3,)),
        ],
        compiler_params=pltpu.CompilerParams(vmem_limit_bytes=56 * 1024 * 1024),
        cost_estimate=pl.CostEstimate(
            flops=0, bytes_accessed=512 * 1024, transcendentals=0
        ),
        name="message",
    )(keys, values, hidden)


def split_kernel(q, up, k, v, mine, send):
    wide = GROUPS * HD
    core = lax.axis_index("core")
    for out, head in ((mine, core), (send, 1 - core)):
        lanes = pl.ds(pl.multiple_of(head * wide, HD), wide)
        out[:, 0:wide] = q[:, lanes]
        out[:, wide : 2 * wide] = up[:, lanes]
        lanes = pl.ds(pl.multiple_of(head * HD, HD), HD)
        out[:, 2 * wide : 2 * wide + HD] = k[:, lanes]
        out[:, 2 * wide + HD :] = v[:, lanes]


def split_heads(q, up, k, v):
    shape = bf16(q.shape[0], 2 * GROUPS * HD + 2 * HD)
    return small_call(split_kernel, "split_heads", [shape, shape], q, up, k, v)


def join_kernel(mine, got, dq, dk, dv):
    wide = GROUPS * HD
    core = lax.axis_index("core")
    for part, head in ((mine, core), (got, 1 - core)):
        dq[:, pl.ds(pl.multiple_of(head * wide, HD), wide)] = part[:, 0:wide]
        lanes = pl.ds(pl.multiple_of(head * HD, HD), HD)
        dk[:, lanes] = part[:, wide : wide + HD]
        dv[:, lanes] = part[:, wide + HD :]


def join_heads(mine, got):
    span = mine.shape[0]
    shapes = [bf16(span, QH * HD), bf16(span, KVH * HD), bf16(span, KVH * HD)]
    return small_call(join_kernel, "join_heads", shapes, mine, got)


def mask_kernel(nz, nzl, slots, span, order_s, order_row, ratio_row, bias):
    x, zh, zl, core = (lax.axis_index(axis) for axis in ("x", "zh", "zl", "core"))
    first = (x * nz + zh * nzl + zl) * CORES
    for r, index in enumerate((first + core, first + 1 - core)):
        owners = visible_bias(order_row[...], ratio_row[...], order_s[index], slots, span)
        for j in range(owners.shape[1]):
            tile = jnp.broadcast_to(owners[:, j : j + 1], (slots, HD))
            bias[r, j * slots : (j + 1) * slots, :] = tile


def mask(order, ratio, nz, nzl, slots, span):
    nseq = order.shape[0]
    return pl.pallas_call(
        functools.partial(mask_kernel, nz, nzl, slots, span),
        in_specs=[SMEM, VMEM, VMEM],
        out_specs=VMEM,
        out_shape=jax.ShapeDtypeStruct((CORES, nseq * slots, HD), F32),
        compiler_params=pltpu.CompilerParams(vmem_limit_bytes=32 * 1024 * 1024),
        cost_estimate=pl.CostEstimate(
            flops=0, bytes_accessed=2 * 1024 * 1024, transcendentals=0
        ),
        name="mask",
    )(order, order.reshape(1, nseq), ratio.reshape(1, nseq))


def turn_kernel(groups, nzh, nzl, slots, got, out):
    count = groups * SUB
    width = nzh * nzl * CORES * slots
    row = lax.broadcasted_iota(jnp.int32, (count, HD), 0)
    lane = lax.broadcasted_iota(jnp.int32, (count, HD), 1)
    same = lane // slots == row // SUB
    from_lane = lax.broadcasted_iota(jnp.int32, (HD, width), 0)
    to_lane = lax.broadcasted_iota(jnp.int32, (HD, width), 1)
    total = jnp.zeros((count, width), F32)
    blocks = got[...].astype(F32)
    for zh in range(nzh):
        for zl in range(nzl):
            for c in range(CORES):
                source = (zh * nzl + zl) * CORES + c
                target = (zl * nzh + zh) * CORES + c
                block = blocks[source * SUB : (source + 1) * SUB, :]
                block = jnp.where(same, jnp.concatenate([block] * groups, axis=0), 0.0)
                put = to_lane == target * slots + from_lane % slots
                total = total + jnp.dot(
                    block.astype(BF16),
                    jnp.where(put, 1.0, 0.0).astype(BF16),
                    preferred_element_type=F32,
                )
    out[...] = total.astype(BF16)


def turn(got, groups, nzh, nzl, slots):
    shape = bf16(groups * SUB, nzh * nzl * CORES * slots)
    kernel = functools.partial(turn_kernel, groups, nzh, nzl, slots)
    return small_call(kernel, "turn", [shape], got)[0]


def zh_kernel(got, out):
    total = add_blocks(got)
    rows = total.shape[0]
    each = rows // out.shape[0]
    keys = total[:, 0:HD].astype(BF16)
    for zh in range(out.shape[0]):
        out[zh, 0:rows, :] = keys
        out[zh, rows:, :] = total[zh * each : (zh + 1) * each, HD:].astype(BF16)


def zh_message(got, nzh):
    _, rows, _ = got.shape
    return small_call(zh_kernel, "zh_message", [bf16(nzh, rows + rows // nzh, HD)], got)[0]


def spread_kernel(got, out):
    total = add_blocks(got).astype(BF16)
    for i in range(out.shape[0]):
        out[i] = total


def spread(got, peers):
    return small_call(spread_kernel, "spread", [bf16(peers, *got.shape[1:])], got)[0]


def weight_kernel(rows, hidden, got, out):
    pairs = []
    for zl in range(got.shape[0] // CORES):
        heads = [got[zl * CORES + c, 0:rows, :] for c in range(CORES)]
        pairs.append(jnp.concatenate(heads, axis=1))
    keys = jnp.concatenate(pairs, axis=0)
    out[...] = jnp.dot(hidden[...], keys, preferred_element_type=F32).astype(BF16)


def weight_terms(hidden, got, rows):
    count, depth = hidden.shape
    return small_call(
        functools.partial(weight_kernel, rows), "weight_terms", [bf16(count, CORES * HD)],
        hidden, got, flops=2 * count * depth * CORES * HD,
    )[0]


def finish_kernel(slots, rows, got, weights, keys, values, weight_grad, held):
    zh, zl, core = (lax.axis_index(axis) for axis in ("zh", "zl", "core"))
    key_row = pl.multiple_of((zh * CORES + core) * slots, slots)
    value_row = pl.multiple_of(rows + core * slots, slots)
    for c in range(CORES):
        held[c] = got[pl.ds(zl * CORES + c, 1)][0].astype(F32)
        lanes = slice(c * HD, (c + 1) * HD)
        keys[:, lanes] = held[c, pl.ds(key_row, slots), :].astype(BF16)
        values[:, lanes] = held[c, pl.ds(value_row, slots), :].astype(BF16)
    weight_grad[...] = add_blocks(weights)[0 : weight_grad.shape[0], :]


def finish(got, weights, slots, rows, rows_out):
    width = weights.shape[2]
    return small_call(
        functools.partial(finish_kernel, slots, rows), "finish",
        [
            bf16(slots, width),
            bf16(slots, width),
            jax.ShapeDtypeStruct((rows_out, width), F32),
        ],
        got, weights, scratch=[pltpu.VMEM((CORES, *got.shape[1:]), F32)],
    )


def near_groups(nx, nzh, nzl):
    groups = []
    for core in range(CORES):
        for zh in range(nzh):
            members = []
            for x in range(nx):
                for zl in range(nzl):
                    place = zh if core == 0 or zl >= nzl // 2 else (zh + 1) % nzh
                    members.append(((x * nzh + place) * nzl + zl) * CORES + core)
            groups.append(members)
    return groups


def per_device(
    nx, nzh, nzl,
    queries, keys, values, grad_out, beacon_keys, beacon_values, beacon_hidden, order, ratio,
):
    ndp = lax.axis_size("dp")
    nz = nzh * nzl
    span = queries.shape[1]
    slots, width = beacon_keys.shape[1:]
    model = beacon_hidden.shape[2]
    groups = ndp * nx
    rows_out = model // (groups * nz * CORES)
    swap = [(0, 1), (1, 0)]

    first = message(beacon_keys[0], beacon_values[0], beacon_hidden[0], groups, nz, rows_out)
    first = first.reshape(nz * CORES, slots, width + HD)
    first = lax.all_to_all(first, ("zh", "zl", "core"), 0, 0, tiled=True)
    mine, send = split_heads(queries[0], grad_out[0], keys[0], values[0])
    other = lax.ppermute(send, "core", swap)
    bias = mask(order, ratio, nz, nzl, slots, span)
    first, mine, other, bias = lax.optimization_barrier((first, mine, other, bias))

    beacons = first[:, :, :width].reshape(1, nz * CORES * slots, width)
    beacons = jnp.broadcast_to(beacons, (nx, nz * CORES * slots, width))
    beacons = lax.all_to_all(beacons, "x", 0, 0, tiled=True)
    beacons = beacons.reshape(nx * nz * CORES * slots, width)

    terms, dscores, probs = attention(bias, mine, other, beacons, nx, nzh, nzl, slots)

    terms = terms.reshape(nx * nzl, nzh * CORES * slots, width)
    terms = lax.all_to_all(
        terms, ("x", "zh", "zl", "core"), 0, 0, tiled=True,
        axis_index_groups=near_groups(nx, nzh, nzl),
    )
    own_out, other_out = own_grads(dscores, probs, mine, other, beacons)
    dq, dk, dv = join_heads(own_out, lax.ppermute(other_out, "core", swap))
    hidden = first[:, :, width:].reshape(nz * CORES * slots, HD)
    hidden = turn(hidden, groups, nzh, nzl, slots)
    terms, hidden, dq, dk, dv = lax.optimization_barrier((terms, hidden, dq, dk, dv))

    terms = lax.all_to_all(zh_message(terms, nzh), "zh", 0, 0, tiled=True)
    terms = lax.all_to_all(spread(terms, nzl * CORES), ("zl", "core"), 0, 0, tiled=True)
    depth = nzh * CORES * slots
    weights = weight_terms(hidden, terms, depth).reshape(groups, SUB, width)
    weights = lax.all_to_all(weights, ("dp", "x"), 0, 0, tiled=True)
    beacon_dk, beacon_dv, weight_grad = finish(terms, weights, slots, depth, rows_out)
    return (dq[None], dk[None], dv[None], beacon_dk[None], beacon_dv[None], weight_grad)


def solution(mesh):
    ndp, nx, nzh, nzl = grid_of(mesh)
    fine = Mesh(
        mesh.devices.reshape(ndp, nx, nzh, nzl, CORES), ("dp", "x", "zh", "zl", "core")
    )
    seq = ("x", "zh", "zl", "core")
    split = P("dp", seq, None)
    return jax.shard_map(
        functools.partial(per_device, nx, nzh, nzl),
        mesh=fine,
        in_specs=(split,) * 7 + (P(), P()),
        out_specs=(split,) * 5 + (P(("dp",) + seq, None),),
        check_vma=False,
    )
```
